256 devices in a mesh: term: 16 (over z, core), doc: 16 (over y, x).
Axes of the slice: x: 4, y: 4, z: 8, core: 2. Of those that a mesh axis runs over, the one named last changes fastest.
Arguments:
- tile_values: bfloat16 [768, 2048, 128], P('term', 'doc'), may hold values from 0.001 to 1, as said below
- tile_rows: int32 [16, 768], P('term', 'doc'), may hold values from 0 to 15, as said below
- tile_cols: int32 [16, 768], P('term', 'doc'), may hold values from 0 to 15, as said below
- tile_count: int32 [16, 16], P('term', 'doc'), may hold values from 16 to 48, as said below
- start_block: bfloat16 [32768, 256], P('doc'), may hold values from -6 to 6
Outputs:
- row_scale: float32 [32768], P('term')
- col_scale: float32 [32768], P('doc')
- left_basis: bfloat16 [32768, 256], P('term')
- right_basis: bfloat16 [32768, 256], P('doc')
The draws below stay inside these ranges and needn't reach their ends.
Inputs may be any that keep to these rules, and one draw needn't show every extreme that they name: `tile_values`: entries are positive. `tile_rows`: within one block pair the occupied (row, column) pairs are distinct, and every tile row and tile column of every block pair holds an occupied tile. `tile_cols`: paired with tile_rows slot by slot. `tile_count`: some block pair has all 48 slots occupied.
All inputs are finite; a program needn't handle non-finite values.
Results may differ from the reference program's by a relative error of at most 0.006.
The reference program's roundings to bfloat16 on the way count: a program that leaves them out, or rounds other values in their place, can miss the bound.
Values may be sent and summed in bfloat16 or wider, within the bound.
No kernel may reach another device: no remote copies, remote signals or barrier semaphores. Data moves between devices by JAX's collectives and lax.ppermute only.
A program may use at most 64 MiB of HBM per device.

```python
import jax
import jax.numpy as jnp
from jax import lax

TILE = 128
K = 256
PASSES = 2
RB = 16
CB = 16
CAP = 48
DOCS = 32768
N_TERM = 16
N_DOC = 16


def draw_tile_values(key, part):
    base = jax.random.fold_in(key, 41)
    entries = jax.random.uniform(base, (N_TERM, CAP, N_DOC, TILE, TILE), jnp.float32, 0.05, 1.0)
    level = jax.random.uniform(jax.random.fold_in(base, 3), (N_TERM, N_DOC), jnp.float32, jnp.log(0.03), 0.0)
    factor = jnp.exp(level)
    scaled = entries * factor[:, None, :, None, None]
    return scaled.reshape(N_TERM * CAP, N_DOC * TILE, TILE).astype(jnp.bfloat16)


def tile_places(key):
    base = jax.random.fold_in(key, 17)
    positions = RB * CB
    scores = jax.random.randint(base, (N_TERM, N_DOC, positions), 0, 1 << 20, dtype=jnp.int32)
    cell = jnp.arange(positions, dtype=jnp.int32)
    row_of = cell // CB
    col_of = cell % CB
    forced = row_of == col_of % RB
    ranked = jnp.where(forced[None, None, :], col_of[None, None, :] - CB, scores * positions + cell[None, None, :])
    order = jnp.argsort(ranked, axis=-1, stable=True)[:, :, :CAP].astype(jnp.int32)
    return (order // CB, order % CB)


def draw_tile_rows(key, part):
    row_part, col_part = tile_places(key)
    return row_part.reshape(N_TERM, N_DOC * CAP)


def draw_tile_cols(key, part):
    row_part, col_part = tile_places(key)
    return col_part.reshape(N_TERM, N_DOC * CAP)


def draw_tile_count(key, part):
    base = jax.random.fold_in(key, 29)
    spread = CAP - CB
    level = jax.random.randint(base, (N_TERM * N_DOC,), 0, spread + 1, dtype=jnp.int32)
    filled = CB + level * level // spread * level // spread
    chosen = jax.random.randint(jax.random.fold_in(base, 1), (), 0, N_TERM * N_DOC, dtype=jnp.int32)
    filled = jnp.where(jnp.arange(N_TERM * N_DOC, dtype=jnp.int32) == chosen, CAP, filled)
    return filled.reshape(N_TERM, N_DOC).astype(jnp.int32)


def block_levels(stream_key, shape, pieces, least, top_value):
    factor_of, own = 1.0, jax.random.fold_in(stream_key, 6)
    for position, parts in pieces:
        draws = jnp.exp(jax.random.uniform(jax.random.fold_in(own, position), (parts,), jnp.float32, least / len(pieces), top_value / len(pieces)))
        factor_of = factor_of * jnp.repeat(draws, shape[position] // parts).reshape([-1 if axis == position else 1 for axis in range(len(shape))])
    return factor_of


def scatter_about(rng, extent, scale, bound, shards=(), kind=jnp.bfloat16):
    loudness = block_levels(rng, extent, shards, -0.22, 0.18) if shards else 1.0
    array = jax.random.normal(rng, extent, jnp.float32) * scale * loudness
    return jnp.minimum(jnp.maximum(array, -bound), bound).astype(kind)


def setup_inputs(seed: int = 0) -> dict:
    arg_keys = jax.random.split(jax.random.key(seed), 6)
    tile_values = draw_tile_values(jax.random.fold_in(arg_keys[5], 71), 0)
    tile_rows = draw_tile_rows(jax.random.fold_in(arg_keys[5], 71), 0)
    tile_cols = draw_tile_cols(jax.random.fold_in(arg_keys[5], 71), 0)
    tile_count = draw_tile_count(jax.random.fold_in(arg_keys[5], 71), 0)
    start_block = scatter_about(arg_keys[4], (DOCS, K), 1.0, 6.0, ((0, 16),))
    return dict(tile_values=tile_values, tile_rows=tile_rows, tile_cols=tile_cols, tile_count=tile_count, start_block=start_block)


PRECISE = lax.Precision.HIGHEST

def factor_inverse(gram):
    lower = jnp.linalg.cholesky(gram)
    identity = jnp.eye(gram.shape[0], dtype=gram.dtype)
    return jax.scipy.linalg.solve_triangular(lower, identity, lower=True).T

def apply_matrix(values, row_ids, col_ids, counts, source, forward):
    width = source.shape[-1]
    if forward:
        out_blocks = RB
    else:
        out_blocks = CB

    def outer_block(outer):

        def inner_step(running, inner):
            if forward:
                term_at, doc_at = (outer, inner)
            else:
                term_at, doc_at = (inner, outer)
            tiles_here = values[term_at, :, doc_at].astype(jnp.float32)
            live_mask = (jnp.arange(CAP, dtype=jnp.int32) < counts[term_at, doc_at]).astype(jnp.float32)
            if forward:
                picked = source[doc_at][col_ids[term_at, doc_at]].astype(jnp.float32)
                product = jnp.einsum('sab,sbk->sak', tiles_here, picked, precision=PRECISE)
                target = row_ids[term_at, doc_at]
            else:
                picked = source[term_at][row_ids[term_at, doc_at]].astype(jnp.float32)
                product = jnp.einsum('sab,sak->sbk', tiles_here, picked, precision=PRECISE)
                target = col_ids[term_at, doc_at]
            product = product * live_mask[:, None, None]
            return (running + jax.ops.segment_sum(product, target, num_segments=out_blocks), None)
        initial = jnp.zeros((out_blocks, TILE, width), jnp.float32)
        inner_total = N_DOC if forward else N_TERM
        return lax.scan(inner_step, initial, jnp.arange(inner_total, dtype=jnp.int32))[0]
    outer_total = N_TERM if forward else N_DOC
    return lax.map(outer_block, jnp.arange(outer_total, dtype=jnp.int32))

def reference(tile_values, tile_rows, tile_cols, tile_count, start_block):
    values = tile_values.reshape(N_TERM, CAP, N_DOC, TILE, TILE)
    row_ids = tile_rows.reshape(N_TERM, N_DOC, CAP).astype(jnp.int32)
    col_ids = tile_cols.reshape(N_TERM, N_DOC, CAP).astype(jnp.int32)
    counts = tile_count.astype(jnp.int32)
    terms_total = N_TERM * RB * TILE
    docs_total = N_DOC * CB * TILE
    col_scale = jnp.ones((N_DOC, CB, TILE, 1), jnp.float32)
    row_scale = jnp.ones((N_TERM, RB, TILE, 1), jnp.float32)
    for sweep_index in range(PASSES):
        row_scale = 1.0 / apply_matrix(values, row_ids, col_ids, counts, col_scale, True)
        col_scale = 1.0 / apply_matrix(values, row_ids, col_ids, counts, row_scale, False)
    row_weight = row_scale * apply_matrix(values, row_ids, col_ids, counts, col_scale, True)
    row_flat = row_scale.reshape(-1, 1)
    col_flat = col_scale.reshape(-1, 1)
    weight_flat = row_weight.reshape(-1)
    start = start_block.astype(jnp.float32)
    start_mean = jnp.sum(start, axis=0)
    scaled_start = (col_flat * start).astype(jnp.bfloat16)
    left_raw = apply_matrix(values, row_ids, col_ids, counts, scaled_start.reshape(N_DOC, CB, TILE, K), True).reshape(-1, K)
    left_block = row_flat * left_raw - weight_flat[:, None] * start_mean[None, :] / docs_total
    left_inverse = factor_inverse(jnp.dot(left_block.T, left_block, precision=PRECISE) / terms_total)
    left_float = jnp.dot(left_block, left_inverse, precision=PRECISE)
    left_basis = left_float.astype(jnp.bfloat16)
    lean = jnp.dot(weight_flat, left_float, precision=PRECISE)
    scaled_left = (row_flat * left_basis.astype(jnp.float32)).astype(jnp.bfloat16)
    right_raw = apply_matrix(values, row_ids, col_ids, counts, scaled_left.reshape(N_TERM, RB, TILE, K), False).reshape(-1, K)
    right_block = col_flat * right_raw - lean[None, :] / docs_total
    right_inverse = factor_inverse(jnp.dot(right_block.T, right_block, precision=PRECISE) / docs_total)
    right_basis = jnp.dot(right_block, right_inverse, precision=PRECISE).astype(jnp.bfloat16)
    return (row_scale.reshape(-1), col_scale.reshape(-1), left_basis, right_basis)
```

```python
import jax
import jax.numpy as jnp
from jax import lax
from jax.experimental import pallas as pl
from jax.experimental.pallas import tpu as pltpu
from jax.sharding import Mesh
from jax.sharding import PartitionSpec as P

TILE = 128
K = 256
RB = 16
CB = 16
CAP = 48
GROUP = 8
PANEL = 64
TERM = ("term_0", "term_1")
DOC = ("doc_0", "doc_1")
ALL = TERM + DOC
F32 = jnp.float32
BF16 = jnp.bfloat16
PRECISE = lax.Precision.HIGHEST
VMEM = pl.BlockSpec(memory_space=pltpu.VMEM)
SMEM = pl.BlockSpec(memory_space=pltpu.SMEM)


def call(body, inputs, outs, scratch=(), flops=1 << 20):
    specs = [SMEM if a.dtype == jnp.int32 else VMEM for a in inputs]
    return pl.pallas_call(
        body,
        out_shape=[jax.ShapeDtypeStruct(s, d) for s, d in outs],
        in_specs=specs,
        out_specs=[VMEM] * len(outs),
        scratch_shapes=[pltpu.VMEM(s, d) for s, d in scratch],
        compiler_params=pltpu.CompilerParams(vmem_limit_bytes=48 * 1024 * 1024),
    )(*inputs)


def thirds(x):
    hi = x.astype(BF16)
    rest = x - hi.astype(F32)
    mid = rest.astype(BF16)
    low = (rest - mid.astype(F32)).astype(BF16)
    return hi, mid, low


def put_thirds(ref, vec, base):
    hi, mid, low = thirds(vec)
    row = lax.broadcasted_iota(jnp.int32, (16, TILE), 0)
    for b in range(RB):
        parts = [jnp.broadcast_to(p[b : b + 1].astype(F32), (16, TILE)) for p in (hi, mid, low)]
        rows = jnp.where(row == 0, parts[0], jnp.where(row == 1, parts[1], jnp.where(row == 2, parts[2], 0.0)))
        ref[b, base : base + 16, :] = rows.astype(BF16)


def over_tiles(count, values, source, target, src_ref, acc_ref, transposed):
    acc_ref[...] = jnp.zeros(acc_ref.shape, F32)
    dims = (((1,), (1,)), ((), ())) if transposed else (((1,), (0,)), ((), ()))

    def visit(g, _):
        products = []
        for u in range(GROUP):
            s = g * GROUP + u
            tile = values[s]
            tile = jnp.where(s < count, tile, jnp.zeros_like(tile))
            products.append(
                lax.dot_general(src_ref[source[0, s]], tile, dims, preferred_element_type=F32)
            )
        for u in range(GROUP):
            s = g * GROUP + u
            acc_ref[target[0, s]] += products[u]
        return 0

    lax.fori_loop(0, (count + GROUP - 1) // GROUP, visit, 0)


def send_vector(out_ref, acc_ref):
    vec = jnp.sum(acc_ref[...], axis=1)
    for i in range(16):
        out_ref[i, 0:RB, :] = vec


def start_sums(values, rows, cols, count, start, out, src, acc):
    put_thirds(src, jnp.ones((CB, TILE), F32), 0)
    over_tiles(count[0, 0], values, cols, rows, src, acc, True)
    send_vector(out, acc)
    mean = jnp.sum(start[...].astype(F32), axis=0, keepdims=True)
    for i in range(16):
        out[i, 16:17, :] = mean[:, :TILE]
        out[i, 17:18, :] = mean[:, TILE:]
        out[i, 18:24, :] = jnp.zeros((6, TILE), F32)


def to_columns(values, rows, cols, count, got, out, scale, src, acc):
    vec = 1.0 / jnp.sum(got[...], axis=0)[0:RB]
    scale[...] = vec
    put_thirds(src, vec, 0)
    over_tiles(count[0, 0], values, rows, cols, src, acc, False)
    send_vector(out, acc)


def to_rows(values, rows, cols, count, got, out, scale, src, acc):
    vec = 1.0 / jnp.sum(got[...], axis=0)[0:RB]
    scale[...] = vec
    put_thirds(src, vec, 0)
    over_tiles(count[0, 0], values, cols, rows, src, acc, True)
    send_vector(out, acc)


def left_product(docs, values, rows, cols, count, got, first, start, out, scale, src, acc):
    vec = 1.0 / jnp.sum(got[...], axis=0)
    scale[...] = vec
    put_thirds(src, vec, K)
    for b in range(CB):
        block = start[b * TILE : (b + 1) * TILE, :].astype(F32).T
        src[b, 0:K, :] = (block * vec[b : b + 1, :]).astype(BF16)
    mean = jnp.sum(first[...], axis=0)[16:18] / docs
    mean = jnp.concatenate([jnp.broadcast_to(mean[h : h + 1], (TILE, TILE)).T for h in range(2)], axis=0)
    over_tiles(count[0, 0], values, cols, rows, src, acc, True)
    for b in range(RB):
        weight = jnp.sum(acc[b, K : K + 16, :], axis=0, keepdims=True)
        out[b] = (acc[b, 0:K, :] - mean * weight).astype(out.dtype)


def left_rows(place, got, row_scale, out, gram):
    d = place[0, 1]
    scale = row_scale[pl.ds(d, 1), :]
    left = scale * jnp.sum(got[...].astype(F32), axis=0)
    sent = (left * scale).astype(BF16)
    for i in range(16):
        out[i] = sent
    gram[...] = lax.dot_general(left, left, (((1,), (1,)), ((), ())), precision=PRECISE, preferred_element_type=F32)


def right_product(values, rows, cols, count, scaled, out, acc):
    over_tiles(count[0, 0], values, rows, cols, scaled, acc, False)
    for b in range(CB):
        out[b] = acc[b].astype(out.dtype)


def iotas(shape=(K, K)):
    return lax.broadcasted_iota(jnp.int32, shape, 0), lax.broadcasted_iota(jnp.int32, shape, 1)


def right_rows(place, got, col_scale, left_gram, out, block):
    t = place[0, 0]
    scale = col_scale[pl.ds(t, 1), :]
    right = scale * jnp.sum(got[...].astype(F32), axis=0)
    block[...] = right
    gram = lax.dot_general(right, right, (((1,), (1,)), ((), ())), precision=PRECISE, preferred_element_type=F32)
    row, col = iotas()
    packed = jnp.where(row >= col, left_gram[...], gram)
    diag = jnp.sum(jnp.where(row == col, gram, 0.0), axis=1, keepdims=True)
    lean = jnp.sum(right, axis=1, keepdims=True)
    lane = lax.broadcasted_iota(jnp.int32, (K, TILE), 1)
    extra = jnp.where(lane == 0, diag, jnp.where(lane == 1, lean, 0.0))
    out[...] = jnp.concatenate([packed, extra], axis=1)


def sum_all(got, out):
    total = jnp.sum(got[...], axis=0, keepdims=True)
    out[...] = jnp.broadcast_to(total, out.shape)


def eliminate(work, start, which):
    first = (start // TILE) * TILE
    width = 3 * TILE
    sub = lax.broadcasted_iota(jnp.int32, (PANEL, 1), 0)
    lane = lax.broadcasted_iota(jnp.int32, (PANEL, TILE), 1)
    lane1 = lax.broadcasted_iota(jnp.int32, (1, TILE), 1)
    step = 4

    def group(g, _):
        base = g * step
        offset = start - first + base
        for m in which:
            panel = work[m, start : start + PANEL, first : first + width]
            head = panel[:, 0:TILE]
            cols = [jnp.sum(jnp.where(lane == offset + a, head, 0.0), axis=1, keepdims=True) for a in range(step)]
            lines = [work[m, pl.ds(start + base + a, 1), first : first + width] for a in range(step)]
            heads = [
                [
                    jnp.sum(jnp.where(lane1 == offset + b, lines[a][:, 0:TILE], 0.0), axis=1, keepdims=True)
                    for b in range(step)
                ]
                for a in range(step)
            ]
            factors = []
            for a in range(step):
                inv = 1.0 / heads[a][a]
                f = jnp.where(sub > base + a, cols[a] * inv, 0.0)
                factors.append(f)
                for b in range(a + 1, step):
                    cols[b] = cols[b] - f * heads[a][b]
                    ratio = heads[b][a] * inv
                    lines[b] = lines[b] - ratio * lines[a]
                    for c in range(a + 1, step):
                        heads[b][c] = heads[b][c] - ratio * heads[a][c]
            for a in range(step):
                panel = panel - factors[a] * lines[a]
            work[m, start : start + PANEL, first : first + width] = panel
        return 0

    lax.fori_loop(0, PANEL // step, group, 0)


def factor(work, which):
    for start in range(0, K, PANEL):
        first = (start // TILE) * TILE
        width = 3 * TILE
        end = start + PANEL
        eliminate(work, start, which)
        for m in which:
            panel = work[m, start:end, first : first + width]
            at = lax.broadcasted_iota(jnp.int32, (PANEL, TILE), 0) + (start - first)
            lane = lax.broadcasted_iota(jnp.int32, (PANEL, TILE), 1)
            pivot = jnp.sum(jnp.where(at == lane, panel[:, 0:TILE], 0.0), axis=1, keepdims=True)
            panel = panel * lax.rsqrt(pivot)
            work[m, start:end, first : first + width] = panel
            if end < K:
                upper = panel[:, end - first : K - first]
                work[m, end:K, first : first + width] -= lax.dot_general(
                    upper, panel, (((0,), (0,)), ((), ())), precision=PRECISE, preferred_element_type=F32
                )


def finish(terms, docs, packed, extra, block, left_inverse, out, work):
    row, col = iotas()
    one = packed[...]
    other = one.T
    e = extra[...]
    lean = e[:, 1:2] / docs
    lean_row = jnp.sum(jnp.where(row == col, lean, 0.0), axis=0, keepdims=True)
    left = jnp.where(row >= col, one, other) / terms
    right = jnp.where(row < col, one, jnp.where(row == col, e[:, 0:1], other)) / docs - lean * lean_row
    eye = jnp.where(row == col, 1.0, 0.0).astype(F32)
    for m, gram in ((0, left), (1, right)):
        work[m, :, 0:K] = gram
        work[m, :, K : 2 * K] = eye
    factor(work, (0, 1))
    inverse = [jnp.where(row >= col, work[m, :, K : 2 * K], 0.0) for m in range(2)]
    left_inverse[...] = inverse[0]
    centred = block[...] - lean
    basis = lax.dot_general(inverse[1], centred, (((1,), (0,)), ((), ())), precision=PRECISE, preferred_element_type=F32)
    basis = basis.T.astype(BF16)
    for i in range(16):
        out[i] = basis


def left_basis_of(inverse, scaled, row_scale, out):
    hi, mid, low = thirds(inverse[...])
    for b in range(RB):
        total = (
            jnp.dot(hi, scaled[b], preferred_element_type=F32)
            + jnp.dot(mid, scaled[b], preferred_element_type=F32)
            + jnp.dot(low, scaled[b], preferred_element_type=F32)
        )
        basis = total / row_scale[b : b + 1, :]
        out[b * TILE : (b + 1) * TILE, :] = basis.T.astype(BF16)


def exchanged(x, axis):
    return lax.all_to_all(x, axis, split_axis=0, concat_axis=0, tiled=True)


WIRE1 = BF16
WIRE2 = F32


def per_device(tile_values, tile_rows, tile_cols, tile_count, start_block):
    terms = float(RB * TILE * lax.axis_size(TERM))
    docs = float(CB * TILE * lax.axis_size(DOC))
    place = jnp.stack([lax.axis_index(TERM), lax.axis_index(DOC)]).astype(jnp.int32)[None]
    tiles = (tile_values, tile_rows, tile_cols, tile_count)
    vec = [((RB, 16, TILE), BF16), ((RB, 16, TILE), F32)]
    vector = ((16, RB, TILE), F32)
    scale = ((RB, TILE), F32)
    (part,) = call(start_sums, (*tiles, start_block), [((16, 24, TILE), F32)], vec)
    first = exchanged(part, DOC)
    part, _ = call(to_columns, (*tiles, first), [vector, scale], vec)
    part, _ = call(to_rows, (*tiles, exchanged(part, TERM)), [vector, scale], vec)
    part, row_scale = call(to_columns, (*tiles, exchanged(part, DOC)), [vector, scale], vec)
    part, col_scale = call(
        lambda *refs: left_product(docs, *refs),
        (*tiles, exchanged(part, TERM), first, start_block),
        [((RB, K, TILE), WIRE1), scale],
        [((CB, K + 16, TILE), BF16), ((RB, K + 16, TILE), F32)],
    )
    part, left_gram = call(
        left_rows, (place, exchanged(part, DOC), row_scale), [((16, K, TILE), BF16), ((K, K), F32)]
    )
    scaled = exchanged(part, DOC)
    (part,) = call(right_product, (*tiles, scaled), [((CB, K, TILE), WIRE2)], [((CB, K, TILE), F32)])
    part, block = call(
        right_rows,
        (place, exchanged(part, TERM), col_scale, left_gram),
        [((K, 3 * TILE), F32), ((K, TILE), F32)],
    )
    part = exchanged(part.reshape(K, 3, TILE), ALL)
    (part,) = call(sum_all, (part,), [((K, 3, TILE), F32)])
    grams = exchanged(part, ALL)
    packed = grams[:, 0:2].reshape(K, K)
    extra = grams[:, 2]
    left_inverse, part = call(
        lambda *refs: finish(terms, docs, *refs),
        (packed, extra, block),
        [((K, K), F32), ((16, TILE, K), BF16)],
        [((2, K, 2 * K), F32)],
    )
    right_basis = exchanged(part, TERM).reshape(CB * TILE, K)
    (left_basis,) = call(left_basis_of, (left_inverse, scaled, row_scale), [((RB * TILE, K), BF16)])
    return (row_scale.reshape(-1), col_scale.reshape(-1), left_basis, right_basis)


def solution(mesh):
    torus = Mesh(mesh.devices.reshape(8, 2, 4, 4), ("term_0", "term_1", "doc_0", "doc_1"))
    placed = (P(TERM, DOC, None), P(TERM, DOC), P(TERM, DOC), P(TERM, DOC), P(DOC, None))
    return jax.shard_map(
        per_device,
        mesh=torus,
        in_specs=placed,
        out_specs=(P(TERM), P(DOC), P(TERM, None), P(DOC, None)),
        check_vma=False,
    )
```

```python
import jax
import jax.numpy as jnp
from jax import lax
from jax.experimental import pallas as pl
from jax.experimental.pallas import tpu as pltpu
from jax.sharding import Mesh
from jax.sharding import PartitionSpec as P

TILE = 128
K = 256
RB = 16
CB = 16
CAP = 48
GROUP = 8
PANEL = 64
TERM = ("term_0", "term_1")
DOC = ("doc_0", "doc_1")
ALL = TERM + DOC
F32 = jnp.float32
BF16 = jnp.bfloat16
PRECISE = lax.Precision.HIGHEST
VMEM = pl.BlockSpec(memory_space=pltpu.VMEM)
SMEM = pl.BlockSpec(memory_space=pltpu.SMEM)


def call(body, inputs, outs, scratch=(), flops=1 << 20):
    specs = [SMEM if a.dtype == jnp.int32 else VMEM for a in inputs]
    return pl.pallas_call(
        body,
        out_shape=[jax.ShapeDtypeStruct(s, d) for s, d in outs],
        in_specs=specs,
        out_specs=[SMEM if d == jnp.int32 else VMEM for _, d in outs],
        scratch_shapes=[pltpu.VMEM(s, d) for s, d in scratch],
        compiler_params=pltpu.CompilerParams(vmem_limit_bytes=16 * 1024 * 1024),
    )(*inputs)


def thirds(x):
    hi = x.astype(BF16)
    rest = x - hi.astype(F32)
    mid = rest.astype(BF16)
    low = (rest - mid.astype(F32)).astype(BF16)
    return hi, mid, low


def put_thirds(ref, vec, base):
    hi, mid, low = thirds(vec)
    row = lax.broadcasted_iota(jnp.int32, (16, TILE), 0)
    for b in range(RB):
        parts = [jnp.broadcast_to(p[b : b + 1].astype(F32), (16, TILE)) for p in (hi, mid, low)]
        rows = jnp.where(row == 0, parts[0], jnp.where(row == 1, parts[1], jnp.where(row == 2, parts[2], 0.0)))
        ref[b, base : base + 16, :] = rows.astype(BF16)


def over_tiles(count, values, source, target, src_ref, acc_ref, transposed):
    acc_ref[...] = jnp.zeros(acc_ref.shape, F32)
    dims = (((1,), (1,)), ((), ())) if transposed else (((1,), (0,)), ((), ()))

    def visit(g, _):
        products = []
        for u in range(GROUP):
            s = g * GROUP + u
            tile = values[s]
            tile = jnp.where(s < count, tile, jnp.zeros_like(tile))
            products.append(
                lax.dot_general(src_ref[source[0, s]], tile, dims, preferred_element_type=F32)
            )
        for u in range(GROUP):
            s = g * GROUP + u
            acc_ref[target[0, s]] += products[u]
        return 0

    lax.fori_loop(0, (count + GROUP - 1) // GROUP, visit, 0)


def send_vector(out_ref, acc_ref):
    vec = jnp.sum(acc_ref[...], axis=1)
    for i in range(16):
        out_ref[i, 0:RB, :] = vec


def start_sums(place, values, rows, cols, count, start, out, place_out, src, acc):
    place_out[0, 0] = place[0, 0]
    place_out[0, 1] = place[0, 1]
    put_thirds(src, jnp.ones((CB, TILE), F32), 0)
    over_tiles(count[0, 0], values, cols, rows, src, acc, True)
    send_vector(out, acc)
    mean = jnp.sum(start[...].astype(F32), axis=0, keepdims=True)
    for i in range(16):
        out[i, 16:17, :] = mean[:, :TILE]
        out[i, 17:18, :] = mean[:, TILE:]
        out[i, 18:24, :] = jnp.zeros((6, TILE), F32)


def to_columns(values, rows, cols, count, got, out, scale, src, acc):
    vec = 1.0 / jnp.sum(got[...], axis=0)[0:RB]
    scale[...] = vec
    put_thirds(src, vec, 0)
    over_tiles(count[0, 0], values, rows, cols, src, acc, False)
    send_vector(out, acc)


def to_rows(values, rows, cols, count, got, out, scale, src, acc):
    vec = 1.0 / jnp.sum(got[...], axis=0)[0:RB]
    scale[...] = vec
    put_thirds(src, vec, 0)
    over_tiles(count[0, 0], values, cols, rows, src, acc, True)
    send_vector(out, acc)


def left_product(docs, values, rows, cols, count, got, first, start, out, scale, src, acc):
    vec = 1.0 / jnp.sum(got[...], axis=0)
    scale[...] = vec
    put_thirds(src, vec, K)
    for b in range(CB):
        block = start[b * TILE : (b + 1) * TILE, :].astype(F32).T
        src[b, 0:K, :] = (block * vec[b : b + 1, :]).astype(BF16)
    mean = jnp.sum(first[...], axis=0)[16:18] / docs
    mean = jnp.concatenate([jnp.broadcast_to(mean[h : h + 1], (TILE, TILE)).T for h in range(2)], axis=0)
    over_tiles(count[0, 0], values, cols, rows, src, acc, True)
    for b in range(RB):
        weight = jnp.sum(acc[b, K : K + 16, :], axis=0, keepdims=True)
        out[b] = (acc[b, 0:K, :] - mean * weight).astype(out.dtype)


def left_rows(place, got, row_scale, out, gram):
    d = place[0, 1]
    scale = row_scale[pl.ds(d, 1), :]
    left = scale * jnp.sum(got[...].astype(F32), axis=0)
    sent = (left * scale).astype(BF16)
    for i in range(16):
        out[i] = sent
    gram[...] = lax.dot_general(left, left, (((1,), (1,)), ((), ())), precision=PRECISE, preferred_element_type=F32)


LEVELS = 32000.0
STEPS = 64.0


def code_of(peak):
    return jnp.ceil(jnp.log2(jnp.maximum(peak, 1e-37)) * STEPS)


def code_lines(code):
    lines = jnp.broadcast_to(code, (K, TILE)).T
    return jnp.concatenate([lines[0:8, :TILE], lines[0:8, TILE:]], axis=0).astype(jnp.int32).astype(jnp.int16)


def counted(x, code):
    steps = x * (jnp.exp2(code * (-1.0 / STEPS)) * LEVELS)
    return jnp.floor(steps + 0.5).astype(jnp.int32).astype(jnp.int16)


def wide(x):
    return x.astype(jnp.int32).astype(F32)


def steps_of(got):
    lines = [wide(got[i, K : K + 16, :]) for i in range(16)]
    code = jnp.concatenate(
        [jnp.concatenate([x[h : h + 1] for x in lines], axis=0) for h in (0, 8)], axis=1
    ).T
    return jnp.exp2(code * (1.0 / STEPS)) * (1.0 / LEVELS)


def right_product(values, rows, cols, count, scaled, col_scale, out, acc):
    over_tiles(count[0, 0], values, rows, cols, scaled, acc, False)
    peak = jnp.zeros((K, TILE), F32)
    for b in range(CB):
        part = acc[b] * col_scale[b : b + 1, :]
        acc[b] = part
        peak = jnp.maximum(peak, jnp.abs(part))
    code = code_of(jnp.max(peak, axis=1, keepdims=True))
    lines = code_lines(code)
    for b in range(CB):
        out[b, 0:K, :] = counted(acc[b], code)
        out[b, K : K + 16, :] = lines


def iotas(shape=(K, K)):
    return lax.broadcasted_iota(jnp.int32, shape, 0), lax.broadcasted_iota(jnp.int32, shape, 1)


def right_rows(got, left_gram, out, own):
    step = steps_of(got)
    right = wide(got[0, 0:K, :]) * step[:, 0:1]
    for i in range(1, 16):
        right += wide(got[i, 0:K, :]) * step[:, i : i + 1]
    code = code_of(jnp.max(jnp.abs(right), axis=1, keepdims=True))
    own[0:K, :] = counted(right, code)
    own[K : K + 16, :] = code_lines(code)
    gram = lax.dot_general(right, right, (((1,), (1,)), ((), ())), precision=PRECISE, preferred_element_type=F32)
    row, col = iotas()
    packed = jnp.where(row >= col, left_gram[...], gram)
    diag = jnp.sum(jnp.where(row == col, gram, 0.0), axis=1, keepdims=True)
    lean = jnp.sum(right, axis=1, keepdims=True)
    lane = lax.broadcasted_iota(jnp.int32, (K, TILE), 1)
    extra = jnp.where(lane == 0, diag, jnp.where(lane == 1, lean, 0.0))
    out[:, 0:K] = packed
    out[:, K : K + TILE] = extra


def sum_all(got, out):
    total = jnp.sum(got[...], axis=0)
    for i in range(16):
        out[i] = total


def eliminate(blocks, at):
    blocks = list(blocks)
    sub = lax.broadcasted_iota(jnp.int32, (8, 1), 0)
    for g in range(len(blocks)):
        lead = blocks[g]
        below = range(g + 1, len(blocks))
        lanes = [at + 8 * g + b for b in range(8)]
        head = [lead[:, l : l + 1] for l in lanes]
        cols = {j: [blocks[j][:, l : l + 1] for l in lanes] for j in below}
        pivots = jnp.ones((8, 1), F32)
        for a in range(8):
            pivot = head[a][a : a + 1]
            inv = 1.0 / pivot
            pivots = jnp.where(sub == a, pivot, pivots)
            line = lead[a : a + 1, :]
            entries = [head[b][a : a + 1] for b in range(8)]
            f = jnp.where(sub > a, head[a] * inv, 0.0)
            lead = lead - f * line
            for b in range(a + 1, 8):
                head[b] = head[b] - f * entries[b]
            for j in below:
                f = cols[j][a] * inv
                blocks[j] = blocks[j] - f * line
                for b in range(a + 1, 8):
                    cols[j][b] = cols[j][b] - f * entries[b]
        blocks[g] = lead * lax.rsqrt(pivots)
    return blocks


def factor(work):
    lane = lax.broadcasted_iota(jnp.int32, (PANEL, TILE), 1)
    line = lax.broadcasted_iota(jnp.int32, (PANEL, TILE), 0)
    for start in range(0, K, PANEL):
        first = (start // TILE) * TILE
        span = slice(first, first + 3 * TILE)
        end = start + PANEL
        at = start - first
        other = PANEL - at
        unit = jnp.where(lane == line + other, 1.0, 0.0)
        here = (lane >= at) & (lane < at + PANEL)
        panels = []
        for m in range(2):
            block = jnp.where(here, work[m, start:end, first : first + TILE], unit)
            panels.append([block[8 * j : 8 * j + 8] for j in range(PANEL // 8)])
        for m, blocks in enumerate(both(panels, at)):
            done = jnp.concatenate(blocks, axis=0)
            inverse = done[:, other : other + PANEL]
            panel = jnp.dot(inverse, work[m, start:end, span], precision=PRECISE, preferred_element_type=F32)
            work[m, start:end, span] = panel
            if end < K:
                work[m, end:K, span] -= lax.dot_general(
                    panel[:, end - first : K - first],
                    panel,
                    (((0,), (0,)), ((), ())),
                    precision=PRECISE,
                    preferred_element_type=F32,
                )


def both(panels, at):
    return [eliminate(p, at) for p in panels]


def finish(terms, docs, grams, inverse, lean_out, work):
    row, col = iotas()
    one = grams[:, 0:K]
    other = one.T
    e = grams[:, K : K + TILE]
    lean = e[:, 1:2] / docs
    lean_row = jnp.sum(jnp.where(row == col, lean, 0.0), axis=0, keepdims=True)
    left = jnp.where(row >= col, one, other) / terms
    right = jnp.where(row < col, one, jnp.where(row == col, e[:, 0:1], other)) / docs - lean * lean_row
    eye = jnp.where(row == col, 1.0, 0.0).astype(F32)
    for m, gram in ((0, left), (1, right)):
        work[m, :, 0:K] = gram
        work[m, :, K : 2 * K] = eye
    factor(work)
    for m in range(2):
        inverse[m] = jnp.where(row >= col, work[m, :, K : 2 * K], 0.0)
    lean_out[...] = jnp.broadcast_to(lean, lean_out.shape)


def bases(inverse, scaled, row_scale, gathered, lean, left_out, right_out):
    hi, mid, low = thirds(inverse[0])
    for b in range(RB):
        total = (
            jnp.dot(hi, scaled[b], preferred_element_type=F32)
            + jnp.dot(mid, scaled[b], preferred_element_type=F32)
            + jnp.dot(low, scaled[b], preferred_element_type=F32)
        )
        basis = total / row_scale[b : b + 1, :]
        left_out[b * TILE : (b + 1) * TILE, :] = basis.T.astype(BF16)
    hi, mid, low = thirds(inverse[1])
    step = steps_of(gathered)
    mean = lean[:, 0:1]
    for b in range(CB):
        block = wide(gathered[b, 0:K, :]) * step[:, b : b + 1] - mean
        top = block.astype(BF16)
        rest = (block - top.astype(F32)).astype(BF16)
        total = (
            jnp.dot(hi, top, preferred_element_type=F32)
            + jnp.dot(mid, top, preferred_element_type=F32)
            + jnp.dot(low, top, preferred_element_type=F32)
            + jnp.dot(hi, rest, preferred_element_type=F32)
            + jnp.dot(mid, rest, preferred_element_type=F32)
        )
        right_out[b * TILE : (b + 1) * TILE, :] = total.T.astype(BF16)


def exchanged(x, axis):
    return lax.all_to_all(x, axis, split_axis=0, concat_axis=0, tiled=True)


def per_device(tile_values, tile_rows, tile_cols, tile_count, start_block):
    terms = float(RB * TILE * lax.axis_size(TERM))
    docs = float(CB * TILE * lax.axis_size(DOC))
    place = jnp.stack([lax.axis_index(TERM), lax.axis_index(DOC)]).astype(jnp.int32)[None]
    tiles = (tile_values, tile_rows, tile_cols, tile_count)
    vec = [((RB, 16, TILE), BF16), ((RB, 16, TILE), F32)]
    vector = ((16, RB, TILE), F32)
    scale = ((RB, TILE), F32)
    part, place = call(
        start_sums, (place, *tiles, start_block), [((16, 24, TILE), F32), ((1, 2), jnp.int32)], vec
    )
    first = exchanged(part, DOC)
    part, _ = call(to_columns, (*tiles, first), [vector, scale], vec)
    part, _ = call(to_rows, (*tiles, exchanged(part, TERM)), [vector, scale], vec)
    part, row_scale = call(to_columns, (*tiles, exchanged(part, DOC)), [vector, scale], vec)
    part, col_scale = call(
        lambda *refs: left_product(docs, *refs),
        (*tiles, exchanged(part, TERM), first, start_block),
        [((RB, K, TILE), BF16), scale],
        [((CB, K + 16, TILE), BF16), ((RB, K + 16, TILE), F32)],
    )
    part, left_gram = call(
        left_rows, (place, exchanged(part, DOC), row_scale), [((16, K, TILE), BF16), ((K, K), F32)]
    )
    scaled = exchanged(part, DOC)
    (part,) = call(
        right_product, (*tiles, scaled, col_scale), [((CB, K + 16, TILE), jnp.int16)], [((CB, K, TILE), F32)]
    )
    part, own = call(
        right_rows,
        (exchanged(part, TERM), left_gram),
        [((K, 3 * TILE), F32), ((K + 16, TILE), jnp.int16)],
    )
    gathered = lax.all_gather(own, TERM)
    spread = [((16, 16, 3 * TILE), F32)]
    part = exchanged(part.reshape(16, 16, 3 * TILE), DOC)
    (part,) = call(sum_all, (part,), spread)
    (part,) = call(sum_all, (exchanged(part, TERM),), spread)
    grams = exchanged(part, DOC).reshape(K, 3 * TILE)
    inverse, lean = call(
        lambda *refs: finish(terms, docs, *refs),
        (grams,),
        [((2, K, K), F32), ((K, TILE), F32)],
        [((2, K, 2 * K), F32)],
    )
    left_basis, right_basis = call(
        bases,
        (inverse, scaled, row_scale, gathered, lean),
        [((RB * TILE, K), BF16), ((CB * TILE, K), BF16)],
    )
    return (row_scale.reshape(-1), col_scale.reshape(-1), left_basis, right_basis)


def solution(mesh):
    torus = Mesh(mesh.devices.reshape(8, 2, 4, 4), ("term_0", "term_1", "doc_0", "doc_1"))
    placed = (P(TERM, DOC, None), P(TERM, DOC), P(TERM, DOC), P(TERM, DOC), P(DOC, None))
    return jax.shard_map(
        per_device,
        mesh=torus,
        in_specs=placed,
        out_specs=(P(TERM), P(DOC), P(TERM, None), P(DOC, None)),
        check_vma=False,
    )
```

```python
import jax
import jax.numpy as jnp
from jax import lax
from jax.experimental import pallas as pl
from jax.experimental.pallas import tpu as pltpu
from jax.sharding import Mesh
from jax.sharding import PartitionSpec as P

TILE = 128
K = 256
RB = 16
CB = 16
CAP = 48
GROUP = 8
PANEL = 64
TERM = ("term_0", "term_1")
DOC = ("doc_0", "doc_1")
ALL = TERM + DOC
F32 = jnp.float32
BF16 = jnp.bfloat16
PRECISE = lax.Precision.HIGHEST
VMEM = pl.BlockSpec(memory_space=pltpu.VMEM)
SMEM = pl.BlockSpec(memory_space=pltpu.SMEM)


def call(body, inputs, outs, scratch=(), flops=1 << 20):
    specs = [SMEM if a.dtype == jnp.int32 else VMEM for a in inputs]
    return pl.pallas_call(
        body,
        out_shape=[jax.ShapeDtypeStruct(s, d) for s, d in outs],
        in_specs=specs,
        out_specs=[SMEM if d == jnp.int32 else VMEM for _, d in outs],
        scratch_shapes=[pltpu.VMEM(s, d) for s, d in scratch],
        compiler_params=pltpu.CompilerParams(vmem_limit_bytes=16 * 1024 * 1024),
    )(*inputs)


def thirds(x):
    hi = x.astype(BF16)
    rest = x - hi.astype(F32)
    mid = rest.astype(BF16)
    low = (rest - mid.astype(F32)).astype(BF16)
    return hi, mid, low


def put_thirds(ref, vec, base):
    hi, mid, low = thirds(vec)
    row = lax.broadcasted_iota(jnp.int32, (16, TILE), 0)
    for b in range(RB):
        parts = [jnp.broadcast_to(p[b : b + 1].astype(F32), (16, TILE)) for p in (hi, mid, low)]
        rows = jnp.where(row == 0, parts[0], jnp.where(row == 1, parts[1], jnp.where(row == 2, parts[2], 0.0)))
        ref[b, base : base + 16, :] = rows.astype(BF16)


def over_tiles(count, values, source, target, src_ref, acc_ref, transposed):
    acc_ref[...] = jnp.zeros(acc_ref.shape, F32)
    dims = (((1,), (1,)), ((), ())) if transposed else (((1,), (0,)), ((), ()))

    def visit(g, _):
        products = []
        for u in range(GROUP):
            s = g * GROUP + u
            tile = values[s]
            tile = jnp.where(s < count, tile, jnp.zeros_like(tile))
            products.append(
                lax.dot_general(src_ref[source[0, s]], tile, dims, preferred_element_type=F32)
            )
        for u in range(GROUP):
            s = g * GROUP + u
            acc_ref[target[0, s]] += products[u]
        return 0

    lax.fori_loop(0, (count + GROUP - 1) // GROUP, visit, 0)


def send_vector(out_ref, acc_ref):
    vec = jnp.sum(acc_ref[...], axis=1)
    for i in range(16):
        out_ref[i, 0:RB, :] = vec


def start_sums(place, values, rows, cols, count, start, out, place_out, src, acc):
    place_out[0, 0] = place[0, 0]
    place_out[0, 1] = place[0, 1]
    put_thirds(src, jnp.ones((CB, TILE), F32), 0)
    over_tiles(count[0, 0], values, cols, rows, src, acc, True)
    send_vector(out, acc)
    mean = jnp.sum(start[...].astype(F32), axis=0, keepdims=True)
    for i in range(16):
        out[i, 16:17, :] = mean[:, :TILE]
        out[i, 17:18, :] = mean[:, TILE:]
        out[i, 18:24, :] = jnp.zeros((6, TILE), F32)


def to_columns(values, rows, cols, count, got, out, scale, src, acc):
    vec = 1.0 / jnp.sum(got[...], axis=0)[0:RB]
    scale[...] = vec
    put_thirds(src, vec, 0)
    over_tiles(count[0, 0], values, rows, cols, src, acc, False)
    send_vector(out, acc)


def to_rows(values, rows, cols, count, got, out, scale, src, acc):
    vec = 1.0 / jnp.sum(got[...], axis=0)[0:RB]
    scale[...] = vec
    put_thirds(src, vec, 0)
    over_tiles(count[0, 0], values, cols, rows, src, acc, True)
    send_vector(out, acc)


def left_product(docs, values, rows, cols, count, got, first, start, out, scale, src, acc):
    vec = 1.0 / jnp.sum(got[...], axis=0)
    scale[...] = vec
    put_thirds(src, vec, K)
    for b in range(CB):
        block = start[b * TILE : (b + 1) * TILE, :].astype(F32).T
        src[b, 0:K, :] = (block * vec[b : b + 1, :]).astype(BF16)
    mean = jnp.sum(first[...], axis=0)[16:18] / docs
    mean = jnp.concatenate([jnp.broadcast_to(mean[h : h + 1], (TILE, TILE)).T for h in range(2)], axis=0)
    over_tiles(count[0, 0], values, cols, rows, src, acc, True)
    for b in range(RB):
        weight = jnp.sum(acc[b, K : K + 16, :], axis=0, keepdims=True)
        out[b] = (acc[b, 0:K, :] - mean * weight).astype(out.dtype)


def left_rows(place, got, row_scale, out, gram):
    d = place[0, 1]
    scale = row_scale[pl.ds(d, 1), :]
    left = scale * jnp.sum(got[...].astype(F32), axis=0)
    sent = (left * scale).astype(BF16)
    for i in range(16):
        out[i] = sent
    gram[...] = lax.dot_general(left, left, (((1,), (1,)), ((), ())), precision=PRECISE, preferred_element_type=F32)


LEVELS = 32000.0
STEPS = 64.0


def code_of(peak):
    return jnp.ceil(jnp.log2(jnp.maximum(peak, 1e-37)) * STEPS)


def code_lines(code):
    lines = jnp.broadcast_to(code, (K, TILE)).T
    return jnp.concatenate([lines[0:8, :TILE], lines[0:8, TILE:]], axis=0).astype(jnp.int32).astype(jnp.int16)


def counted(x, code):
    steps = x * (jnp.exp2(code * (-1.0 / STEPS)) * LEVELS)
    return jnp.floor(steps + 0.5).astype(jnp.int32).astype(jnp.int16)


def wide(x):
    return x.astype(jnp.int32).astype(F32)


def steps_of(got):
    lines = [wide(got[i, K : K + 16, :]) for i in range(16)]
    code = jnp.concatenate(
        [jnp.concatenate([x[h : h + 1] for x in lines], axis=0) for h in (0, 8)], axis=1
    ).T
    return jnp.exp2(code * (1.0 / STEPS)) * (1.0 / LEVELS)


def right_product(values, rows, cols, count, scaled, col_scale, out, acc):
    over_tiles(count[0, 0], values, rows, cols, scaled, acc, False)
    peak = jnp.zeros((K, TILE), F32)
    for b in range(CB):
        part = acc[b] * col_scale[b : b + 1, :]
        acc[b] = part
        peak = jnp.maximum(peak, jnp.abs(part))
    code = code_of(jnp.max(peak, axis=1, keepdims=True))
    lines = code_lines(code)
    for b in range(CB):
        out[b, 0:K, :] = counted(acc[b], code)
        out[b, K : K + 16, :] = lines


def iotas(shape=(K, K)):
    return lax.broadcasted_iota(jnp.int32, shape, 0), lax.broadcasted_iota(jnp.int32, shape, 1)


def right_rows(got, left_gram, out, own):
    step = steps_of(got)
    right = wide(got[0, 0:K, :]) * step[:, 0:1]
    for i in range(1, 16):
        right += wide(got[i, 0:K, :]) * step[:, i : i + 1]
    code = code_of(jnp.max(jnp.abs(right), axis=1, keepdims=True))
    own[0:K, :] = counted(right, code)
    own[K : K + 16, :] = code_lines(code)
    gram = lax.dot_general(right, right, (((1,), (1,)), ((), ())), precision=PRECISE, preferred_element_type=F32)
    row, col = iotas()
    packed = jnp.where(row >= col, left_gram[...], gram)
    diag = jnp.sum(jnp.where(row == col, gram, 0.0), axis=1, keepdims=True)
    lean = jnp.sum(right, axis=1, keepdims=True)
    lane = lax.broadcasted_iota(jnp.int32, (K, TILE), 1)
    extra = jnp.where(lane == 0, diag, jnp.where(lane == 1, lean, 0.0))
    out[:, 0:K] = packed
    out[:, K : K + TILE] = extra


def sum_all(got, out):
    total = jnp.sum(got[...], axis=0)
    for i in range(16):
        out[i] = total


def spread(x, lane):
    return jnp.broadcast_to(x[:, :, lane : lane + 1], x.shape)


def eliminate(blocks, at):
    blocks = list(blocks)
    sub = lax.broadcasted_iota(jnp.int32, (2, 8, TILE), 1)
    for g in range(len(blocks)):
        lead = blocks[g]
        lanes = [at + 8 * g + b for b in range(8)]
        head = [spread(lead, l) for l in lanes]
        pivots = jnp.ones((2, 8, TILE), F32)
        lines, inverses, entries = [], [], []
        for a in range(8):
            pivot = head[a][:, a : a + 1]
            inv = 1.0 / pivot
            line = lead[:, a : a + 1]
            entry = [head[b][:, a : a + 1] for b in range(8)]
            lines.append(line)
            inverses.append(inv)
            entries.append(entry)
            pivots = jnp.where(sub == a, pivot, pivots)
            f = jnp.where(sub > a, head[a] * inv, 0.0)
            lead = lead - f * line
            for b in range(a + 1, 8):
                head[b] = head[b] - f * entry[b]
        for j in range(g + 1, len(blocks)):
            cols = [spread(blocks[j], l) for l in lanes]
            total = blocks[j]
            for a in range(8):
                f = cols[a] * inverses[a]
                total = total - f * lines[a]
                for b in range(a + 1, 8):
                    cols[b] = cols[b] - f * entries[a][b]
            blocks[j] = total
        blocks[g] = lead * lax.rsqrt(pivots)
    return blocks


def factor(work):
    lane = lax.broadcasted_iota(jnp.int32, (2, PANEL, TILE), 2)
    line = lax.broadcasted_iota(jnp.int32, (2, PANEL, TILE), 1)
    for start in range(0, K, PANEL):
        first = (start // TILE) * TILE
        span = slice(first, first + 3 * TILE)
        end = start + PANEL
        at = start - first
        other = PANEL - at
        unit = jnp.where(lane == line + other, 1.0, 0.0)
        here = (lane >= at) & (lane < at + PANEL)
        block = jnp.where(here, work[:, start:end, first : first + TILE], unit)
        done = jnp.concatenate(eliminate([block[:, 8 * j : 8 * j + 8] for j in range(PANEL // 8)], at), axis=1)
        for m in range(2):
            inverse = done[m, :, other : other + PANEL]
            panel = jnp.dot(inverse, work[m, start:end, span], precision=PRECISE, preferred_element_type=F32)
            work[m, start:end, span] = panel
            if end < K:
                work[m, end:K, span] -= lax.dot_general(
                    panel[:, end - first : K - first],
                    panel,
                    (((0,), (0,)), ((), ())),
                    precision=PRECISE,
                    preferred_element_type=F32,
                )


def finish(terms, docs, grams, inverse, lean_out, work):
    row, col = iotas()
    one = grams[:, 0:K]
    other = one.T
    e = grams[:, K : K + TILE]
    lean = e[:, 1:2] / docs
    lean_row = jnp.sum(jnp.where(row == col, lean, 0.0), axis=0, keepdims=True)
    left = jnp.where(row >= col, one, other) / terms
    right = jnp.where(row < col, one, jnp.where(row == col, e[:, 0:1], other)) / docs - lean * lean_row
    eye = jnp.where(row == col, 1.0, 0.0).astype(F32)
    for m, gram in ((0, left), (1, right)):
        work[m, :, 0:K] = gram
        work[m, :, K : 2 * K] = eye
    factor(work)
    for m in range(2):
        inverse[m] = jnp.where(row >= col, work[m, :, K : 2 * K], 0.0)
    lean_out[...] = jnp.broadcast_to(lean, lean_out.shape)


def bases(inverse, scaled, row_scale, gathered, lean, left_out, right_out):
    hi, mid, low = thirds(inverse[0])
    for b in range(RB):
        total = (
            jnp.dot(hi, scaled[b], preferred_element_type=F32)
            + jnp.dot(mid, scaled[b], preferred_element_type=F32)
            + jnp.dot(low, scaled[b], preferred_element_type=F32)
        )
        basis = total / row_scale[b : b + 1, :]
        left_out[b * TILE : (b + 1) * TILE, :] = basis.T.astype(BF16)
    hi, mid, low = thirds(inverse[1])
    step = steps_of(gathered)
    mean = lean[:, 0:1]
    for b in range(CB):
        block = wide(gathered[b, 0:K, :]) * step[:, b : b + 1] - mean
        top = block.astype(BF16)
        rest = (block - top.astype(F32)).astype(BF16)
        total = (
            jnp.dot(hi, top, preferred_element_type=F32)
            + jnp.dot(mid, top, preferred_element_type=F32)
            + jnp.dot(low, top, preferred_element_type=F32)
            + jnp.dot(hi, rest, preferred_element_type=F32)
            + jnp.dot(mid, rest, preferred_element_type=F32)
        )
        right_out[b * TILE : (b + 1) * TILE, :] = total.T.astype(BF16)


def exchanged(x, axis):
    return lax.all_to_all(x, axis, split_axis=0, concat_axis=0, tiled=True)


def per_device(tile_values, tile_rows, tile_cols, tile_count, start_block):
    terms = float(RB * TILE * lax.axis_size(TERM))
    docs = float(CB * TILE * lax.axis_size(DOC))
    place = jnp.stack([lax.axis_index(TERM), lax.axis_index(DOC)]).astype(jnp.int32)[None]
    tiles = (tile_values, tile_rows, tile_cols, tile_count)
    vec = [((RB, 16, TILE), BF16), ((RB, 16, TILE), F32)]
    vector = ((16, RB, TILE), F32)
    scale = ((RB, TILE), F32)
    part, place = call(
        start_sums, (place, *tiles, start_block), [((16, 24, TILE), F32), ((1, 2), jnp.int32)], vec
    )
    first = exchanged(part, DOC)
    part, _ = call(to_columns, (*tiles, first), [vector, scale], vec)
    part, _ = call(to_rows, (*tiles, exchanged(part, TERM)), [vector, scale], vec)
    part, row_scale = call(to_columns, (*tiles, exchanged(part, DOC)), [vector, scale], vec)
    part, col_scale = call(
        lambda *refs: left_product(docs, *refs),
        (*tiles, exchanged(part, TERM), first, start_block),
        [((RB, K, TILE), BF16), scale],
        [((CB, K + 16, TILE), BF16), ((RB, K + 16, TILE), F32)],
    )
    part, left_gram = call(
        left_rows, (place, exchanged(part, DOC), row_scale), [((16, K, TILE), BF16), ((K, K), F32)]
    )
    scaled = exchanged(part, DOC)
    (part,) = call(
        right_product, (*tiles, scaled, col_scale), [((CB, K + 16, TILE), jnp.int16)], [((CB, K, TILE), F32)]
    )
    part, own = call(
        right_rows,
        (exchanged(part, TERM), left_gram),
        [((K, 3 * TILE), F32), ((K + 16, TILE), jnp.int16)],
    )
    gathered = lax.all_gather(own, TERM)
    spread = [((16, 16, 3 * TILE), F32)]
    part = exchanged(part.reshape(16, 16, 3 * TILE), DOC)
    (part,) = call(sum_all, (part,), spread)
    (part,) = call(sum_all, (exchanged(part, TERM),), spread)
    grams = exchanged(part, DOC).reshape(K, 3 * TILE)
    inverse, lean = call(
        lambda *refs: finish(terms, docs, *refs),
        (grams,),
        [((2, K, K), F32), ((K, TILE), F32)],
        [((2, K, 2 * K), F32)],
    )
    left_basis, right_basis = call(
        bases,
        (inverse, scaled, row_scale, gathered, lean),
        [((RB * TILE, K), BF16), ((CB * TILE, K), BF16)],
    )
    return (row_scale.reshape(-1), col_scale.reshape(-1), left_basis, right_basis)


def solution(mesh):
    torus = Mesh(mesh.devices.reshape(8, 2, 4, 4), ("term_0", "term_1", "doc_0", "doc_1"))
    placed = (P(TERM, DOC, None), P(TERM, DOC), P(TERM, DOC), P(TERM, DOC), P(DOC, None))
    return jax.shard_map(
        per_device,
        mesh=torus,
        in_specs=placed,
        out_specs=(P(TERM), P(DOC), P(TERM, None), P(DOC, None)),
        check_vma=False,
    )
```

```python
import jax
import jax.numpy as jnp
from jax import lax
from jax.experimental import pallas as pl
from jax.experimental.pallas import tpu as pltpu
from jax.sharding import Mesh
from jax.sharding import PartitionSpec as P

TILE = 128
K = 256
RB = 16
CB = 16
CAP = 48
GROUP = 8
PANEL = 64
TERM = ("term_0", "term_1")
DOC = ("doc_0", "doc_1")
ALL = TERM + DOC
F32 = jnp.float32
BF16 = jnp.bfloat16
PRECISE = lax.Precision.HIGHEST
VMEM = pl.BlockSpec(memory_space=pltpu.VMEM)
SMEM = pl.BlockSpec(memory_space=pltpu.SMEM)


def call(body, inputs, outs, scratch=(), flops=1 << 20):
    specs = [SMEM if a.dtype == jnp.int32 else VMEM for a in inputs]
    return pl.pallas_call(
        body,
        out_shape=[jax.ShapeDtypeStruct(s, d) for s, d in outs],
        in_specs=specs,
        out_specs=[SMEM if d == jnp.int32 else VMEM for _, d in outs],
        scratch_shapes=[pltpu.VMEM(s, d) for s, d in scratch],
        compiler_params=pltpu.CompilerParams(vmem_limit_bytes=16 * 1024 * 1024),
    )(*inputs)


def thirds(x):
    hi = x.astype(BF16)
    rest = x - hi.astype(F32)
    mid = rest.astype(BF16)
    low = (rest - mid.astype(F32)).astype(BF16)
    return hi, mid, low


def put_thirds(ref, vec, base):
    hi, mid, low = thirds(vec)
    row = lax.broadcasted_iota(jnp.int32, (16, TILE), 0)
    for b in range(RB):
        parts = [jnp.broadcast_to(p[b : b + 1].astype(F32), (16, TILE)) for p in (hi, mid, low)]
        rows = jnp.where(row == 0, parts[0], jnp.where(row == 1, parts[1], jnp.where(row == 2, parts[2], 0.0)))
        ref[b, base : base + 16, :] = rows.astype(BF16)


def over_tiles(count, values, source, target, src_ref, acc_ref, transposed):
    acc_ref[...] = jnp.zeros(acc_ref.shape, F32)
    dims = (((1,), (1,)), ((), ())) if transposed else (((1,), (0,)), ((), ()))

    def visit(g, _):
        products = []
        for u in range(GROUP):
            s = g * GROUP + u
            tile = values[s]
            tile = jnp.where(s < count, tile, jnp.zeros_like(tile))
            products.append(
                lax.dot_general(src_ref[source[0, s]], tile, dims, preferred_element_type=F32)
            )
        for u in range(GROUP):
            s = g * GROUP + u
            acc_ref[target[0, s]] += products[u]
        return 0

    lax.fori_loop(0, (count + GROUP - 1) // GROUP, visit, 0)


def send_vector(out_ref, acc_ref):
    vec = jnp.sum(acc_ref[...], axis=1)
    for i in range(16):
        out_ref[i, 0:RB, :] = vec


def first_rows(place, values, rows, cols, count, out, place_out, src, acc):
    for i in range(3):
        place_out[0, i] = place[0, i]
    put_thirds(src, jnp.ones((CB, TILE), F32), 0)
    over_tiles(count[0, 0], values, cols, rows, src, acc, True)
    send_vector(out, acc)


def to_columns(values, rows, cols, count, got, out, scale, src, acc):
    vec = 1.0 / jnp.sum(got[...], axis=0)[0:RB]
    scale[...] = vec
    put_thirds(src, vec, 0)
    over_tiles(count[0, 0], values, rows, cols, src, acc, False)
    send_vector(out, acc)


def to_rows(values, rows, cols, count, got, start, out, src, acc):
    put_thirds(src, 1.0 / jnp.sum(got[...], axis=0), 0)
    over_tiles(count[0, 0], values, cols, rows, src, acc, True)
    send_vector(out, acc)
    mean = jnp.sum(start[...].astype(F32), axis=0, keepdims=True)
    for i in range(16):
        out[i, 16:17, :] = mean[:, :TILE]
        out[i, 17:18, :] = mean[:, TILE:]
        out[i, 18:24, :] = jnp.zeros((6, TILE), F32)


def left_product(docs, values, rows, cols, count, got, first, start, out, scale, src, acc):
    vec = 1.0 / jnp.sum(got[...], axis=0)
    scale[...] = vec
    put_thirds(src, vec, K)
    for b in range(CB):
        block = start[b * TILE : (b + 1) * TILE, :].astype(F32).T
        src[b, 0:K, :] = (block * vec[b : b + 1, :]).astype(BF16)
    mean = jnp.sum(first[...], axis=0)[16:18] / docs
    mean = jnp.concatenate([jnp.broadcast_to(mean[h : h + 1], (TILE, TILE)).T for h in range(2)], axis=0)
    over_tiles(count[0, 0], values, cols, rows, src, acc, True)
    for b in range(RB):
        weight = jnp.sum(acc[b, K : K + 16, :], axis=0, keepdims=True)
        out[b] = (acc[b, 0:K, :] - mean * weight).astype(out.dtype)


def left_rows(place, got, row_scale, out, gram):
    d = place[0, 1]
    scale = row_scale[pl.ds(d, 1), :]
    left = scale * jnp.sum(got[...].astype(F32), axis=0)
    sent = (left * scale).astype(BF16)
    for i in range(16):
        out[i] = sent
    gram[...] = lax.dot_general(left, left, (((1,), (1,)), ((), ())), precision=PRECISE, preferred_element_type=F32)


LEVELS = 32000.0
STEPS = 64.0


def code_of(peak):
    return jnp.ceil(jnp.log2(jnp.maximum(peak, 1e-37)) * STEPS)


def code_lines(code):
    lines = jnp.broadcast_to(code, (K, TILE)).T
    return jnp.concatenate([lines[0:8, :TILE], lines[0:8, TILE:]], axis=0).astype(jnp.int32).astype(jnp.int16)


def counted(x, code):
    steps = x * (jnp.exp2(code * (-1.0 / STEPS)) * LEVELS)
    return jnp.floor(steps + 0.5).astype(jnp.int32).astype(jnp.int16)


def wide(x):
    return x.astype(jnp.int32).astype(F32)


def steps_of(got, count):
    lines = [wide(got[i, K : K + 16, :]) for i in range(count)]
    code = jnp.concatenate(
        [jnp.concatenate([x[h : h + 1] for x in lines], axis=0) for h in (0, 8)], axis=1
    ).T
    return jnp.exp2(code * (1.0 / STEPS)) * (1.0 / LEVELS)


def right_product(place, values, rows, cols, count, scaled, col_scale, keep, send, acc):
    over_tiles(count[0, 0], values, rows, cols, scaled, acc, False)
    core = place[0, 2]
    peak = jnp.zeros((K, TILE), F32)
    for i in range(CB // 2):
        mine, its = 2 * i + core, 2 * i + 1 - core
        keep[i] = acc[mine] * col_scale[pl.ds(mine, 1), :]
        part = acc[its] * col_scale[pl.ds(its, 1), :]
        acc[its] = part
        peak = jnp.maximum(peak, jnp.abs(part))
    code = code_of(jnp.max(peak, axis=1, keepdims=True))
    lines = code_lines(code)
    for i in range(CB // 2):
        send[i, 0:K, :] = counted(acc[2 * i + 1 - core], code)
        send[i, K : K + 16, :] = lines


def core_sum(keep, got, out, total):
    step = steps_of(got, 8)[:, 0:1]
    peak = jnp.zeros((K, TILE), F32)
    for i in range(CB // 2):
        part = keep[i] + wide(got[i, 0:K, :]) * step
        total[i] = part
        peak = jnp.maximum(peak, jnp.abs(part))
    code = code_of(jnp.max(peak, axis=1, keepdims=True))
    lines = code_lines(code)
    for i in range(CB // 2):
        out[i, 0:K, :] = counted(total[i], code)
        out[i, K : K + 16, :] = lines


def iotas(shape=(K, K)):
    return lax.broadcasted_iota(jnp.int32, shape, 0), lax.broadcasted_iota(jnp.int32, shape, 1)


def right_rows(got, left_gram, out, own):
    step = steps_of(got, 8)
    right = wide(got[0, 0:K, :]) * step[:, 0:1]
    for i in range(1, 8):
        right += wide(got[i, 0:K, :]) * step[:, i : i + 1]
    code = code_of(jnp.max(jnp.abs(right), axis=1, keepdims=True))
    own[0:K, :] = counted(right, code)
    own[K : K + 16, :] = code_lines(code)
    gram = lax.dot_general(right, right, (((1,), (1,)), ((), ())), precision=PRECISE, preferred_element_type=F32)
    row, col = iotas()
    packed = jnp.where(row >= col, left_gram[...], gram)
    diag = jnp.sum(jnp.where(row == col, gram, 0.0), axis=1, keepdims=True)
    lean = jnp.sum(right, axis=1, keepdims=True)
    lane = lax.broadcasted_iota(jnp.int32, (K, TILE), 1)
    extra = jnp.where(lane == 0, diag, jnp.where(lane == 1, lean, 0.0))
    out[:, 0:K] = packed
    out[:, K : K + TILE] = extra


def sum_all(got, out):
    total = jnp.sum(got[...], axis=0)
    for i in range(16):
        out[i] = total


def spread(x, lane):
    return jnp.broadcast_to(x[:, :, lane : lane + 1], x.shape)


def eliminate(blocks, at):
    blocks = list(blocks)
    sub = lax.broadcasted_iota(jnp.int32, (2, 8, TILE), 1)
    for g in range(len(blocks)):
        lead = blocks[g]
        lanes = [at + 8 * g + b for b in range(8)]
        head = [spread(lead, l) for l in lanes]
        pivots = jnp.ones((2, 8, TILE), F32)
        lines, inverses, entries = [], [], []
        for a in range(8):
            pivot = head[a][:, a : a + 1]
            inv = 1.0 / pivot
            line = lead[:, a : a + 1]
            entry = [head[b][:, a : a + 1] for b in range(8)]
            lines.append(line)
            inverses.append(inv)
            entries.append(entry)
            pivots = jnp.where(sub == a, pivot, pivots)
            f = jnp.where(sub > a, head[a] * inv, 0.0)
            lead = lead - f * line
            for b in range(a + 1, 8):
                head[b] = head[b] - f * entry[b]
        for j in range(g + 1, len(blocks)):
            cols = [spread(blocks[j], l) for l in lanes]
            total = blocks[j]
            for a in range(8):
                f = cols[a] * inverses[a]
                total = total - f * lines[a]
                for b in range(a + 1, 8):
                    cols[b] = cols[b] - f * entries[a][b]
            blocks[j] = total
        blocks[g] = lead * lax.rsqrt(pivots)
    return blocks


def factor(work):
    lane = lax.broadcasted_iota(jnp.int32, (2, PANEL, TILE), 2)
    line = lax.broadcasted_iota(jnp.int32, (2, PANEL, TILE), 1)
    for start in range(0, K, PANEL):
        first = (start // TILE) * TILE
        span = slice(first, first + 3 * TILE)
        end = start + PANEL
        at = start - first
        other = PANEL - at
        unit = jnp.where(lane == line + other, 1.0, 0.0)
        here = (lane >= at) & (lane < at + PANEL)
        block = jnp.where(here, work[:, start:end, first : first + TILE], unit)
        done = jnp.concatenate(eliminate([block[:, 8 * j : 8 * j + 8] for j in range(PANEL // 8)], at), axis=1)
        for m in range(2):
            inverse = done[m, :, other : other + PANEL]
            panel = jnp.dot(inverse, work[m, start:end, span], precision=PRECISE, preferred_element_type=F32)
            work[m, start:end, span] = panel
            if end < K:
                work[m, end:K, span] -= lax.dot_general(
                    panel[:, end - first : K - first],
                    panel,
                    (((0,), (0,)), ((), ())),
                    precision=PRECISE,
                    preferred_element_type=F32,
                )


def finish(terms, docs, grams, inverse, lean_out, work):
    row, col = iotas()
    one = grams[:, 0:K]
    other = one.T
    e = grams[:, K : K + TILE]
    lean = e[:, 1:2] / docs
    lean_row = jnp.sum(jnp.where(row == col, lean, 0.0), axis=0, keepdims=True)
    left = jnp.where(row >= col, one, other) / terms
    right = jnp.where(row < col, one, jnp.where(row == col, e[:, 0:1], other)) / docs - lean * lean_row
    eye = jnp.where(row == col, 1.0, 0.0).astype(F32)
    for m, gram in ((0, left), (1, right)):
        work[m, :, 0:K] = gram
        work[m, :, K : 2 * K] = eye
    factor(work)
    for m in range(2):
        inverse[m] = jnp.where(row >= col, work[m, :, K : 2 * K], 0.0)
    lean_out[...] = jnp.broadcast_to(lean, lean_out.shape)


def halves(x):
    hi = x.astype(BF16)
    return hi, (x - hi.astype(F32)).astype(BF16)


def mixed(lhs, rhs):
    return sum(jnp.dot(a, b, preferred_element_type=F32) for a, b in zip(lhs, rhs))


def bases(inverse, scaled, row_scale, gathered, lean, left_out, right_out):
    hi, low = halves(inverse[0])
    for b in range(0, RB, 2):
        pair = jnp.concatenate([scaled[b], scaled[b + 1]], axis=1)
        total = mixed((hi, low), (pair, pair))
        for u in range(2):
            basis = total[:, u * TILE : (u + 1) * TILE] / row_scale[b + u : b + u + 1, :]
            left_out[(b + u) * TILE : (b + u + 1) * TILE, :] = basis.T.astype(BF16)
    hi, low = halves(inverse[1])
    step = steps_of(gathered, 16)
    mean = lean[:, 0:1]
    for b in range(0, CB, 2):
        pair = jnp.concatenate(
            [wide(gathered[b + u, 0:K, :]) * step[:, b + u : b + u + 1] - mean for u in range(2)], axis=1
        )
        top, rest = halves(pair)
        total = mixed((hi, low, hi), (top, top, rest))
        for u in range(2):
            right_out[(b + u) * TILE : (b + u + 1) * TILE, :] = total[:, u * TILE : (u + 1) * TILE].T.astype(BF16)


def exchanged(x, axis):
    return lax.all_to_all(x, axis, split_axis=0, concat_axis=0, tiled=True)


def per_device(tile_values, tile_rows, tile_cols, tile_count, start_block):
    terms = float(RB * TILE * lax.axis_size(TERM))
    docs = float(CB * TILE * lax.axis_size(DOC))
    place = jnp.stack([lax.axis_index(TERM), lax.axis_index(DOC), lax.axis_index("term_1")]).astype(jnp.int32)[None]
    tiles = (tile_values, tile_rows, tile_cols, tile_count)
    vec = [((RB, 16, TILE), BF16), ((RB, 16, TILE), F32)]
    vector = ((16, RB, TILE), F32)
    scale = ((RB, TILE), F32)
    part, place = call(first_rows, (place, *tiles), [vector, ((1, 3), jnp.int32)], vec)
    part, _ = call(to_columns, (*tiles, exchanged(part, DOC)), [vector, scale], vec)
    (part,) = call(to_rows, (*tiles, exchanged(part, TERM), start_block), [((16, 24, TILE), F32)], vec)
    first = exchanged(part, DOC)
    part, row_scale = call(to_columns, (*tiles, first), [vector, scale], vec)
    part, col_scale = call(
        lambda *refs: left_product(docs, *refs),
        (*tiles, exchanged(part, TERM), first, start_block),
        [((RB, K, TILE), BF16), scale],
        [((CB, K + 16, TILE), BF16), ((RB, K + 16, TILE), F32)],
    )
    part, left_gram = call(
        left_rows, (place, exchanged(part, DOC), row_scale), [((16, K, TILE), BF16), ((K, K), F32)]
    )
    scaled = exchanged(part, DOC)
    half = (CB // 2, K + 16, TILE)
    keep, part = call(
        right_product,
        (place, *tiles, scaled, col_scale),
        [((CB // 2, K, TILE), F32), (half, jnp.int16)],
        [((CB, K, TILE), F32)],
    )
    part = lax.ppermute(part, "term_1", [(0, 1), (1, 0)])
    (part,) = call(core_sum, (keep, part), [(half, jnp.int16)], [((CB // 2, K, TILE), F32)])
    part, own = call(
        right_rows,
        (exchanged(part, "term_0"), left_gram),
        [((K, 3 * TILE), F32), ((K + 16, TILE), jnp.int16)],
    )
    gathered = lax.all_gather(own, TERM)
    spread = [((16, 16, 3 * TILE), F32)]
    part = exchanged(part.reshape(16, 16, 3 * TILE), DOC)
    (part,) = call(sum_all, (part,), spread)
    (part,) = call(sum_all, (exchanged(part, TERM),), spread)
    grams = exchanged(part, DOC).reshape(K, 3 * TILE)
    inverse, lean = call(
        lambda *refs: finish(terms, docs, *refs),
        (grams,),
        [((2, K, K), F32), ((K, TILE), F32)],
        [((2, K, 2 * K), F32)],
    )
    left_basis, right_basis = call(
        bases,
        (inverse, scaled, row_scale, gathered, lean),
        [((RB * TILE, K), BF16), ((CB * TILE, K), BF16)],
    )
    return (row_scale.reshape(-1), col_scale.reshape(-1), left_basis, right_basis)


def solution(mesh):
    torus = Mesh(mesh.devices.reshape(8, 2, 4, 4), ("term_0", "term_1", "doc_0", "doc_1"))
    placed = (P(TERM, DOC, None), P(TERM, DOC), P(TERM, DOC), P(TERM, DOC), P(DOC, None))
    return jax.shard_map(
        per_device,
        mesh=torus,
        in_specs=placed,
        out_specs=(P(TERM), P(DOC), P(TERM, None), P(DOC, None)),
        check_vma=False,
    )
```

```python
import jax
import jax.numpy as jnp
from jax import lax
from jax.experimental import pallas as pl
from jax.experimental.pallas import tpu as pltpu
from jax.sharding import Mesh
from jax.sharding import PartitionSpec as P

TILE = 128
K = 256
RB = 16
CB = 16
CAP = 48
GROUP = 8
PANEL = 64
TERM = ("term_0", "term_1")
DOC = ("doc_0", "doc_1")
PLANE = ("term_1",) + DOC
F32 = jnp.float32
BF16 = jnp.bfloat16
PRECISE = lax.Precision.HIGHEST
VMEM = pl.BlockSpec(memory_space=pltpu.VMEM)
SMEM = pl.BlockSpec(memory_space=pltpu.SMEM)


def call(body, inputs, outs, scratch=(), flops=1 << 20):
    specs = [SMEM if a.dtype == jnp.int32 else VMEM for a in inputs]
    return pl.pallas_call(
        body,
        out_shape=[jax.ShapeDtypeStruct(s, d) for s, d in outs],
        in_specs=specs,
        out_specs=[SMEM if d == jnp.int32 else VMEM for _, d in outs],
        scratch_shapes=[pltpu.VMEM(s, d) for s, d in scratch],
        compiler_params=pltpu.CompilerParams(vmem_limit_bytes=16 * 1024 * 1024),
    )(*inputs)


def thirds(x):
    hi = x.astype(BF16)
    rest = x - hi.astype(F32)
    mid = rest.astype(BF16)
    low = (rest - mid.astype(F32)).astype(BF16)
    return hi, mid, low


def put_thirds(ref, vec, base):
    hi, mid, low = thirds(vec)
    row = lax.broadcasted_iota(jnp.int32, (16, TILE), 0)
    for b in range(RB):
        parts = [jnp.broadcast_to(p[b : b + 1].astype(F32), (16, TILE)) for p in (hi, mid, low)]
        rows = jnp.where(row == 0, parts[0], jnp.where(row == 1, parts[1], jnp.where(row == 2, parts[2], 0.0)))
        ref[b, base : base + 16, :] = rows.astype(BF16)


def over_tiles(count, values, source, target, src_ref, acc_ref, transposed):
    acc_ref[...] = jnp.zeros(acc_ref.shape, F32)
    dims = (((1,), (1,)), ((), ())) if transposed else (((1,), (0,)), ((), ()))

    def visit(g, _):
        products = []
        for u in range(GROUP):
            s = g * GROUP + u
            tile = values[s]
            tile = jnp.where(s < count, tile, jnp.zeros_like(tile))
            products.append(
                lax.dot_general(src_ref[source[0, s]], tile, dims, preferred_element_type=F32)
            )
        for u in range(GROUP):
            s = g * GROUP + u
            acc_ref[target[0, s]] += products[u]
        return 0

    lax.fori_loop(0, (count + GROUP - 1) // GROUP, visit, 0)


def send_vector(out_ref, acc_ref):
    vec = jnp.sum(acc_ref[...], axis=1)
    for i in range(16):
        out_ref[i, 0:RB, :] = vec


def first_rows(place, values, rows, cols, count, out, place_out, src, acc):
    for i in range(3):
        place_out[0, i] = place[0, i]
    put_thirds(src, jnp.ones((CB, TILE), F32), 0)
    over_tiles(count[0, 0], values, cols, rows, src, acc, True)
    send_vector(out, acc)


def to_columns(values, rows, cols, count, got, out, scale, src, acc):
    vec = 1.0 / jnp.sum(got[...], axis=0)[0:RB]
    scale[...] = vec
    put_thirds(src, vec, 0)
    over_tiles(count[0, 0], values, rows, cols, src, acc, False)
    send_vector(out, acc)


def to_rows(values, rows, cols, count, got, start, out, src, acc):
    put_thirds(src, 1.0 / jnp.sum(got[...], axis=0), 0)
    over_tiles(count[0, 0], values, cols, rows, src, acc, True)
    send_vector(out, acc)
    mean = jnp.sum(start[...].astype(F32), axis=0, keepdims=True)
    for i in range(16):
        out[i, 16:17, :] = mean[:, :TILE]
        out[i, 17:18, :] = mean[:, TILE:]
        out[i, 18:24, :] = jnp.zeros((6, TILE), F32)


def left_product(docs, values, rows, cols, count, got, first, start, out, scale, src, acc):
    vec = 1.0 / jnp.sum(got[...], axis=0)
    scale[...] = vec
    put_thirds(src, vec, K)
    for b in range(CB):
        block = start[b * TILE : (b + 1) * TILE, :].astype(F32).T
        src[b, 0:K, :] = (block * vec[b : b + 1, :]).astype(BF16)
    mean = jnp.sum(first[...], axis=0)[16:18] / docs
    mean = jnp.concatenate([jnp.broadcast_to(mean[h : h + 1], (TILE, TILE)).T for h in range(2)], axis=0)
    over_tiles(count[0, 0], values, cols, rows, src, acc, True)
    for b in range(RB):
        weight = jnp.sum(acc[b, K : K + 16, :], axis=0, keepdims=True)
        out[b] = (acc[b, 0:K, :] - mean * weight).astype(out.dtype)


def left_rows(place, got, row_scale, out, gram):
    d = place[0, 1]
    scale = row_scale[pl.ds(d, 1), :]
    left = scale * jnp.sum(got[...].astype(F32), axis=0)
    sent = (left * scale).astype(BF16)
    for i in range(16):
        out[i] = sent
    gram[...] = lax.dot_general(left, left, (((1,), (1,)), ((), ())), precision=PRECISE, preferred_element_type=F32)


LEVELS = 32000.0
STEPS = 64.0


def code_of(peak):
    return jnp.ceil(jnp.log2(jnp.maximum(peak, 1e-37)) * STEPS)


def code_lines(code):
    lines = jnp.broadcast_to(code, (K, TILE)).T
    return jnp.concatenate([lines[0:8, :TILE], lines[0:8, TILE:]], axis=0).astype(jnp.int32).astype(jnp.int16)


def counted(x, code):
    steps = x * (jnp.exp2(code * (-1.0 / STEPS)) * LEVELS)
    return jnp.floor(steps + 0.5).astype(jnp.int32).astype(jnp.int16)


def wide(x):
    return x.astype(jnp.int32).astype(F32)


def steps_of(got, count):
    lines = [wide(got[i, K : K + 16, :]) for i in range(count)]
    code = jnp.concatenate(
        [jnp.concatenate([x[h : h + 1] for x in lines], axis=0) for h in (0, 8)], axis=1
    ).T
    return jnp.exp2(code * (1.0 / STEPS)) * (1.0 / LEVELS)


def right_product(place, values, rows, cols, count, scaled, col_scale, keep, send, acc):
    over_tiles(count[0, 0], values, rows, cols, scaled, acc, False)
    core = place[0, 2]
    peak = jnp.zeros((K, TILE), F32)
    for i in range(CB // 2):
        mine, its = 2 * i + core, 2 * i + 1 - core
        keep[i] = acc[mine] * col_scale[pl.ds(mine, 1), :]
        part = acc[its] * col_scale[pl.ds(its, 1), :]
        acc[its] = part
        peak = jnp.maximum(peak, jnp.abs(part))
    code = code_of(jnp.max(peak, axis=1, keepdims=True))
    lines = code_lines(code)
    for i in range(CB // 2):
        send[i, 0:K, :] = counted(acc[2 * i + 1 - core], code)
        send[i, K : K + 16, :] = lines


def core_sum(keep, got, out, total):
    step = steps_of(got, 8)[:, 0:1]
    peak = jnp.zeros((K, TILE), F32)
    for i in range(CB // 2):
        part = keep[i] + wide(got[i, 0:K, :]) * step
        total[i] = part
        peak = jnp.maximum(peak, jnp.abs(part))
    code = code_of(jnp.max(peak, axis=1, keepdims=True))
    lines = code_lines(code)
    for i in range(CB // 2):
        out[i, 0:K, :] = counted(total[i], code)
        out[i, K : K + 16, :] = lines


def iotas(shape=(K, K)):
    return lax.broadcasted_iota(jnp.int32, shape, 0), lax.broadcasted_iota(jnp.int32, shape, 1)


def right_rows(got, left_gram, out, own):
    step = steps_of(got, 8)
    right = wide(got[0, 0:K, :]) * step[:, 0:1]
    for i in range(1, 8):
        right += wide(got[i, 0:K, :]) * step[:, i : i + 1]
    code = code_of(jnp.max(jnp.abs(right), axis=1, keepdims=True))
    own[0:K, :] = counted(right, code)
    own[K : K + 16, :] = code_lines(code)
    gram = lax.dot_general(right, right, (((1,), (1,)), ((), ())), precision=PRECISE, preferred_element_type=F32)
    row, col = iotas()
    packed = jnp.where(row >= col, left_gram[...], gram)
    diag = jnp.sum(jnp.where(row == col, gram, 0.0), axis=1, keepdims=True)
    lean = jnp.sum(right, axis=1, keepdims=True)
    lane = lax.broadcasted_iota(jnp.int32, (K, TILE), 1)
    extra = jnp.where(lane == 0, diag, jnp.where(lane == 1, lean, 0.0))
    out[:, 0:K] = packed
    out[:, K : K + TILE] = extra


def sum_all(got, out):
    total = jnp.sum(got[...], axis=0)
    for i in range(out.shape[0]):
        out[i] = total


def spread(x, lane):
    return jnp.broadcast_to(x[:, :, lane : lane + 1], x.shape)


def eliminate(blocks, at):
    blocks = list(blocks)
    sub = lax.broadcasted_iota(jnp.int32, (2, 8, TILE), 1)
    for g in range(len(blocks)):
        lead = blocks[g]
        lanes = [at + 8 * g + b for b in range(8)]
        head = [spread(lead, l) for l in lanes]
        pivots = jnp.ones((2, 8, TILE), F32)
        lines, inverses, entries = [], [], []
        for a in range(8):
            pivot = head[a][:, a : a + 1]
            inv = 1.0 / pivot
            line = lead[:, a : a + 1]
            entry = [head[b][:, a : a + 1] for b in range(8)]
            lines.append(line)
            inverses.append(inv)
            entries.append(entry)
            pivots = jnp.where(sub == a, pivot, pivots)
            f = jnp.where(sub > a, head[a] * inv, 0.0)
            lead = lead - f * line
            for b in range(a + 1, 8):
                head[b] = head[b] - f * entry[b]
        for j in range(g + 1, len(blocks)):
            cols = [spread(blocks[j], l) for l in lanes]
            total = blocks[j]
            for a in range(8):
                f = cols[a] * inverses[a]
                total = total - f * lines[a]
                for b in range(a + 1, 8):
                    cols[b] = cols[b] - f * entries[a][b]
            blocks[j] = total
        blocks[g] = lead * lax.rsqrt(pivots)
    return blocks


def precise(lhs, rhs, contract=1):
    return lax.dot_general(lhs, rhs, (((contract,), (0,)), ((), ())), precision=PRECISE, preferred_element_type=F32)


def factor(work):
    lane = lax.broadcasted_iota(jnp.int32, (2, PANEL, TILE), 2)
    line = lax.broadcasted_iota(jnp.int32, (2, PANEL, TILE), 1)
    own = work[:, 0:PANEL, 0:TILE]
    for start in range(0, K, PANEL):
        first = (start // TILE) * TILE
        span = slice(first, first + 3 * TILE)
        end = start + PANEL
        at = start - first
        other = PANEL - at
        unit = jnp.where(lane == line + other, 1.0, 0.0)
        here = (lane >= at) & (lane < at + PANEL)
        block = jnp.where(here, own, unit)
        done = jnp.concatenate(eliminate([block[:, 8 * j : 8 * j + 8] for j in range(PANEL // 8)], at), axis=1)
        inverses = [done[m, :, other : other + PANEL] for m in range(2)]
        if end < K:
            then = (end // TILE) * TILE
            ahead = []
            for m in range(2):
                upper = precise(inverses[m], work[m, start:end, then : then + TILE])
                cut = upper[:, end - then : end - then + PANEL]
                ahead.append(work[m, end : end + PANEL, then : then + TILE] - precise(cut, upper, 0))
            own = jnp.stack(ahead)
        for m in range(2):
            panel = precise(inverses[m], work[m, start:end, span])
            work[m, start:end, span] = panel
            if end < K:
                work[m, end:K, span] -= precise(panel[:, end - first : K - first], panel, 0)


def finish(terms, docs, grams, inverse, lean_out, work):
    row, col = iotas()
    one = grams[:, 0:K]
    other = one.T
    e = grams[:, K : K + TILE]
    lean = e[:, 1:2] / docs
    lean_row = jnp.sum(jnp.where(row == col, lean, 0.0), axis=0, keepdims=True)
    left = jnp.where(row >= col, one, other) / terms
    right = jnp.where(row < col, one, jnp.where(row == col, e[:, 0:1], other)) / docs - lean * lean_row
    eye = jnp.where(row == col, 1.0, 0.0).astype(F32)
    for m, gram in ((0, left), (1, right)):
        work[m, :, 0:K] = gram
        work[m, :, K : 2 * K] = eye
    factor(work)
    for m in range(2):
        inverse[m] = jnp.where(row >= col, work[m, :, K : 2 * K], 0.0)
    lean_out[...] = jnp.broadcast_to(lean, lean_out.shape)


def halves(x):
    hi = x.astype(BF16)
    return hi, (x - hi.astype(F32)).astype(BF16)


def mixed(lhs, rhs):
    return sum(jnp.dot(a, b, preferred_element_type=F32) for a, b in zip(lhs, rhs))


def bases(inverse, scaled, row_scale, gathered, lean, left_out, right_out):
    hi, low = halves(inverse[0])
    for b in range(0, RB, 2):
        pair = jnp.concatenate([scaled[b], scaled[b + 1]], axis=1)
        total = mixed((hi, low), (pair, pair))
        for u in range(2):
            basis = total[:, u * TILE : (u + 1) * TILE] / row_scale[b + u : b + u + 1, :]
            left_out[(b + u) * TILE : (b + u + 1) * TILE, :] = basis.T.astype(BF16)
    hi, low = halves(inverse[1])
    step = steps_of(gathered, 16)
    mean = lean[:, 0:1]
    for b in range(0, CB, 2):
        pair = jnp.concatenate(
            [wide(gathered[b + u, 0:K, :]) * step[:, b + u : b + u + 1] - mean for u in range(2)], axis=1
        )
        top, rest = halves(pair)
        total = mixed((hi, low, hi), (top, top, rest))
        for u in range(2):
            right_out[(b + u) * TILE : (b + u + 1) * TILE, :] = total[:, u * TILE : (u + 1) * TILE].T.astype(BF16)


def exchanged(x, axis):
    return lax.all_to_all(x, axis, split_axis=0, concat_axis=0, tiled=True)


def per_device(tile_values, tile_rows, tile_cols, tile_count, start_block):
    terms = float(RB * TILE * lax.axis_size(TERM))
    docs = float(CB * TILE * lax.axis_size(DOC))
    place = jnp.stack([lax.axis_index(TERM), lax.axis_index(DOC), lax.axis_index("term_1")]).astype(jnp.int32)[None]
    tiles = (tile_values, tile_rows, tile_cols, tile_count)
    vec = [((RB, 16, TILE), BF16), ((RB, 16, TILE), F32)]
    vector = ((16, RB, TILE), F32)
    scale = ((RB, TILE), F32)
    part, place = call(first_rows, (place, *tiles), [vector, ((1, 3), jnp.int32)], vec)
    part, _ = call(to_columns, (*tiles, exchanged(part, DOC)), [vector, scale], vec)
    (part,) = call(to_rows, (*tiles, exchanged(part, TERM), start_block), [((16, 24, TILE), F32)], vec)
    first = exchanged(part, DOC)
    part, row_scale = call(to_columns, (*tiles, first), [vector, scale], vec)
    part, col_scale = call(
        lambda *refs: left_product(docs, *refs),
        (*tiles, exchanged(part, TERM), first, start_block),
        [((RB, K, TILE), BF16), scale],
        [((CB, K + 16, TILE), BF16), ((RB, K + 16, TILE), F32)],
    )
    part, left_gram = call(
        left_rows, (place, exchanged(part, DOC), row_scale), [((16, K, TILE), BF16), ((K, K), F32)]
    )
    scaled = exchanged(part, DOC)
    half = (CB // 2, K + 16, TILE)
    keep, part = call(
        right_product,
        (place, *tiles, scaled, col_scale),
        [((CB // 2, K, TILE), F32), (half, jnp.int16)],
        [((CB, K, TILE), F32)],
    )
    part = lax.ppermute(part, "term_1", [(0, 1), (1, 0)])
    (part,) = call(core_sum, (keep, part), [(half, jnp.int16)], [((CB // 2, K, TILE), F32)])
    part, own = call(
        right_rows,
        (exchanged(part, "term_0"), left_gram),
        [((K, 3 * TILE), F32), ((K + 16, TILE), jnp.int16)],
    )
    gathered = lax.all_gather(own, TERM)
    part = exchanged(part.reshape(32, 8, 3 * TILE), PLANE)
    (part,) = call(sum_all, (part,), [((8, 8, 3 * TILE), F32)])
    (part,) = call(sum_all, (exchanged(part, "term_0"),), [((32, 8, 3 * TILE), F32)])
    grams = exchanged(part, PLANE).reshape(K, 3 * TILE)
    inverse, lean = call(
        lambda *refs: finish(terms, docs, *refs),
        (grams,),
        [((2, K, K), F32), ((K, TILE), F32)],
        [((2, K, 2 * K), F32)],
    )
    left_basis, right_basis = call(
        bases,
        (inverse, scaled, row_scale, gathered, lean),
        [((RB * TILE, K), BF16), ((CB * TILE, K), BF16)],
    )
    return (row_scale.reshape(-1), col_scale.reshape(-1), left_basis, right_basis)


def solution(mesh):
    torus = Mesh(mesh.devices.reshape(8, 2, 4, 4), ("term_0", "term_1", "doc_0", "doc_1"))
    placed = (P(TERM, DOC, None), P(TERM, DOC), P(TERM, DOC), P(TERM, DOC), P(DOC, None))
    return jax.shard_map(
        per_device,
        mesh=torus,
        in_specs=placed,
        out_specs=(P(TERM), P(DOC), P(TERM, None), P(DOC, None)),
        check_vma=False,
    )
```

```python
import jax
import jax.numpy as jnp
from jax import lax
from jax.experimental import pallas as pl
from jax.experimental.pallas import tpu as pltpu
from jax.sharding import Mesh
from jax.sharding import PartitionSpec as P

TILE = 128
K = 256
RB = 16
CB = 16
CAP = 48
GROUP = 24
PANEL = 64
TERM = ("term_0", "term_1")
DOC = ("doc_0", "doc_1")
PLANE = ("term_1",) + DOC
F32 = jnp.float32
BF16 = jnp.bfloat16
PRECISE = lax.Precision.HIGHEST
VMEM = pl.BlockSpec(memory_space=pltpu.VMEM)
SMEM = pl.BlockSpec(memory_space=pltpu.SMEM)


def call(body, inputs, outs, scratch=(), specs=None, mib=16):
    return pl.pallas_call(
        body,
        out_shape=[jax.ShapeDtypeStruct(s, d) for s, d in outs],
        in_specs=specs or [SMEM if a.dtype == jnp.int32 else VMEM for a in inputs],
        out_specs=[VMEM] * len(outs),
        scratch_shapes=[pltpu.VMEM(s[0], s[1]) if isinstance(s, tuple) else s for s in scratch],
        compiler_params=pltpu.CompilerParams(vmem_limit_bytes=int(mib * 1024 * 1024)),
    )(*inputs)


def thirds(x):
    hi = x.astype(BF16)
    rest = x - hi.astype(F32)
    mid = rest.astype(BF16)
    low = (rest - mid.astype(F32)).astype(BF16)
    return hi, mid, low


def put_thirds(ref, vec, base):
    hi, mid, low = thirds(vec)
    row = lax.broadcasted_iota(jnp.int32, (16, TILE), 0)
    for b in range(RB):
        parts = [jnp.broadcast_to(p[b : b + 1].astype(F32), (16, TILE)) for p in (hi, mid, low)]
        rows = jnp.where(row == 0, parts[0], jnp.where(row == 1, parts[1], jnp.where(row == 2, parts[2], 0.0)))
        ref[b, base : base + 16, :] = rows.astype(BF16)


def over_tiles(count, values, source, target, src_ref, acc_ref, transposed, group, ready=None):
    acc_ref[...] = jnp.zeros(acc_ref.shape, F32)
    dims = (((1,), (1,)), ((), ())) if transposed else (((1,), (0,)), ((), ()))

    def visit(g, _):
        products = []
        for u in range(group):
            s = g * group + u
            tile = values[s]
            tile = jnp.where(s < count, tile, jnp.zeros_like(tile))
            products.append(
                lax.dot_general(src_ref[source[0, s]], tile, dims, preferred_element_type=F32)
            )
        for u in range(group):
            s = g * group + u
            acc_ref[target[0, s]] += products[u]
        return 0

    if ready is None and group < CAP:
        lax.fori_loop(0, (count + group - 1) // group, visit, 0)
        return
    for g in range(CAP // group):
        if ready is not None:
            ready(g)
        visit(g, 0)


def send_vector(out_ref, acc_ref):
    vec = jnp.sum(acc_ref[...], axis=1)
    for i in range(16):
        out_ref[i, 0:RB, :] = vec


def first_rows(values_in, rows_in, cols_in, count, out, src, acc, values, rows, cols, sems):
    parts = CAP // GROUP
    copies = [pltpu.make_async_copy(rows_in, rows, sems.at[0]), pltpu.make_async_copy(cols_in, cols, sems.at[1])]
    for g in range(parts):
        own = pl.ds(g * GROUP, GROUP)
        copies.append(pltpu.make_async_copy(values_in.at[own], values.at[own], sems.at[2 + g]))
    for copy in copies:
        copy.start()
    put_thirds(src, jnp.ones((CB, TILE), F32), 0)
    copies[0].wait()
    copies[1].wait()
    over_tiles(count[0, 0], values, cols, rows, src, acc, True, GROUP, lambda g: copies[2 + g].wait())
    send_vector(out, acc)


def to_columns(values, rows, cols, count, got, out, scale, src, acc):
    vec = 1.0 / jnp.sum(got[...], axis=0)[0:RB]
    scale[...] = vec
    put_thirds(src, vec, 0)
    over_tiles(count[0, 0], values, rows, cols, src, acc, False, CAP)
    send_vector(out, acc)


def to_rows(values, rows, cols, count, got, start, out, src, acc):
    put_thirds(src, 1.0 / jnp.sum(got[...], axis=0), 0)
    over_tiles(count[0, 0], values, cols, rows, src, acc, True, GROUP)
    send_vector(out, acc)
    mean = jnp.sum(start[...].astype(F32), axis=0, keepdims=True)
    for i in range(16):
        out[i, 16:17, :] = mean[:, :TILE]
        out[i, 17:18, :] = mean[:, TILE:]
        out[i, 18:24, :] = jnp.zeros((6, TILE), F32)


def left_product(docs, values, rows, cols, count, got, first, start, out, scale, src, acc):
    vec = 1.0 / jnp.sum(got[...], axis=0)
    scale[...] = vec
    put_thirds(src, vec, K)
    for b in range(CB):
        block = start[b * TILE : (b + 1) * TILE, :].T.astype(F32)
        src[b, 0:K, :] = (block * vec[b : b + 1, :]).astype(BF16)
    mean = jnp.sum(first[...], axis=0)[16:18] / docs
    mean = jnp.concatenate([jnp.broadcast_to(mean[h : h + 1], (TILE, TILE)).T for h in range(2)], axis=0)
    over_tiles(count[0, 0], values, cols, rows, src, acc, True, GROUP)
    for b in range(RB):
        weight = jnp.sum(acc[b, K : K + 16, :], axis=0, keepdims=True)
        out[b] = (acc[b, 0:K, :] - mean * weight).astype(out.dtype)


def left_rows(got, row_scale, out, gram):
    d = lax.axis_index(DOC)
    scale = row_scale[pl.ds(d, 1), :]
    left = scale * jnp.sum(got[...].astype(F32), axis=0)
    sent = (left * scale).astype(BF16)
    for i in range(16):
        out[i] = sent
    gram[...] = lax.dot_general(left, left, (((1,), (1,)), ((), ())), precision=PRECISE, preferred_element_type=F32)


LEVELS = 32000.0
STEPS = 64.0


def code_of(peak):
    return jnp.ceil(jnp.log2(jnp.maximum(peak, 1e-37)) * STEPS)


def code_lines(code):
    lines = jnp.broadcast_to(code, (K, TILE)).T
    return jnp.concatenate([lines[0:8, :TILE], lines[0:8, TILE:]], axis=0).astype(jnp.int32).astype(jnp.int16)


def counted(x, code):
    steps = x * (jnp.exp2(code * (-1.0 / STEPS)) * LEVELS)
    return jnp.floor(steps + 0.5).astype(jnp.int32).astype(jnp.int16)


def wide(x):
    return x.astype(jnp.int32).astype(F32)


def steps_of(got, count):
    lines = [wide(got[i, K : K + 16, :]) for i in range(count)]
    code = jnp.concatenate(
        [jnp.concatenate([x[h : h + 1] for x in lines], axis=0) for h in (0, 8)], axis=1
    ).T
    return jnp.exp2(code * (1.0 / STEPS)) * (1.0 / LEVELS)


def right_product(values, rows, cols, count, scaled, col_scale, keep, send, acc):
    over_tiles(count[0, 0], values, rows, cols, scaled, acc, False, GROUP)
    core = lax.axis_index("term_1")
    peak = jnp.zeros((K, TILE), F32)
    for i in range(CB // 2):
        mine, its = 2 * i + core, 2 * i + 1 - core
        keep[i] = acc[mine] * col_scale[pl.ds(mine, 1), :]
        part = acc[its] * col_scale[pl.ds(its, 1), :]
        acc[its] = part
        peak = jnp.maximum(peak, jnp.abs(part))
    code = code_of(jnp.max(peak, axis=1, keepdims=True))
    lines = code_lines(code)
    for i in range(CB // 2):
        send[i, 0:K, :] = counted(acc[2 * i + 1 - core], code)
        send[i, K : K + 16, :] = lines


def core_sum(keep, got, out, total):
    step = steps_of(got, 8)[:, 0:1]
    peak = jnp.zeros((K, TILE), F32)
    for i in range(CB // 2):
        part = keep[i] + wide(got[i, 0:K, :]) * step
        total[i] = part
        peak = jnp.maximum(peak, jnp.abs(part))
    code = code_of(jnp.max(peak, axis=1, keepdims=True))
    lines = code_lines(code)
    for i in range(CB // 2):
        out[i, 0:K, :] = counted(total[i], code)
        out[i, K : K + 16, :] = lines


def iotas(shape=(K, K)):
    return lax.broadcasted_iota(jnp.int32, shape, 0), lax.broadcasted_iota(jnp.int32, shape, 1)


def right_rows(got, left_gram, out, own):
    step = steps_of(got, 8)
    right = wide(got[0, 0:K, :]) * step[:, 0:1]
    for i in range(1, 8):
        right += wide(got[i, 0:K, :]) * step[:, i : i + 1]
    code = code_of(jnp.max(jnp.abs(right), axis=1, keepdims=True))
    own[0:K, :] = counted(right, code)
    own[K : K + 16, :] = code_lines(code)
    gram = lax.dot_general(right, right, (((1,), (1,)), ((), ())), precision=PRECISE, preferred_element_type=F32)
    row, col = iotas()
    packed = jnp.where(row >= col, left_gram[...], gram)
    diag = jnp.sum(jnp.where(row == col, gram, 0.0), axis=1, keepdims=True)
    lean = jnp.sum(right, axis=1, keepdims=True)
    lane = lax.broadcasted_iota(jnp.int32, (K, TILE), 1)
    extra = jnp.where(lane == 0, diag, jnp.where(lane == 1, lean, 0.0))
    out[:, 0:K] = packed
    out[:, K : K + TILE] = extra


def sum_all(got, out):
    total = jnp.sum(got[...], axis=0)
    for i in range(out.shape[0]):
        out[i] = total


def spread(x, lane):
    return jnp.broadcast_to(x[:, :, lane : lane + 1], x.shape)


def eliminate(blocks, at):
    blocks = list(blocks)
    sub = lax.broadcasted_iota(jnp.int32, (2, 8, TILE), 1)
    for g in range(len(blocks)):
        lead = blocks[g]
        lanes = [at + 8 * g + b for b in range(8)]
        head = [spread(lead, l) for l in lanes]
        pivots = jnp.ones((2, 8, TILE), F32)
        lines, inverses, entries = [], [], []
        for a in range(8):
            pivot = head[a][:, a : a + 1]
            inv = 1.0 / pivot
            line = lead[:, a : a + 1]
            entry = [head[b][:, a : a + 1] for b in range(8)]
            lines.append(line)
            inverses.append(inv)
            entries.append(entry)
            pivots = jnp.where(sub == a, pivot, pivots)
            f = jnp.where(sub > a, head[a] * inv, 0.0)
            lead = lead - f * line
            for b in range(a + 1, 8):
                head[b] = head[b] - f * entry[b]
        for j in range(g + 1, len(blocks)):
            cols = [spread(blocks[j], l) for l in lanes]
            total = blocks[j]
            for a in range(8):
                f = cols[a] * inverses[a]
                total = total - f * lines[a]
                for b in range(a + 1, 8):
                    cols[b] = cols[b] - f * entries[a][b]
            blocks[j] = total
        blocks[g] = lead * lax.rsqrt(pivots)
    return blocks


def precise(lhs, rhs, contract=1):
    return lax.dot_general(lhs, rhs, (((contract,), (0,)), ((), ())), precision=PRECISE, preferred_element_type=F32)


def factor(work):
    lane = lax.broadcasted_iota(jnp.int32, (2, PANEL, TILE), 2)
    line = lax.broadcasted_iota(jnp.int32, (2, PANEL, TILE), 1)
    own = work[:, 0:PANEL, 0:TILE]
    for start in range(0, K, PANEL):
        first = (start // TILE) * TILE
        span = slice(first, first + 3 * TILE)
        end = start + PANEL
        at = start - first
        other = PANEL - at
        unit = jnp.where(lane == line + other, 1.0, 0.0)
        here = (lane >= at) & (lane < at + PANEL)
        block = jnp.where(here, own, unit)
        done = jnp.concatenate(eliminate([block[:, 8 * j : 8 * j + 8] for j in range(PANEL // 8)], at), axis=1)
        inverses = [done[m, :, other : other + PANEL] for m in range(2)]
        if end < K:
            then = (end // TILE) * TILE
            ahead = []
            for m in range(2):
                upper = precise(inverses[m], work[m, start:end, then : then + TILE])
                cut = upper[:, end - then : end - then + PANEL]
                ahead.append(work[m, end : end + PANEL, then : then + TILE] - precise(cut, upper, 0))
            own = jnp.stack(ahead)
        for m in range(2):
            panel = precise(inverses[m], work[m, start:end, span])
            work[m, start:end, span] = panel
            if end < K:
                work[m, end:K, span] -= precise(panel[:, end - first : K - first], panel, 0)


def finish(terms, docs, grams, inverse, lean_out, work):
    row, col = iotas()
    one = grams[:, 0:K]
    other = one.T
    e = grams[:, K : K + TILE]
    lean = e[:, 1:2] / docs
    lean_row = jnp.sum(jnp.where(row == col, lean, 0.0), axis=0, keepdims=True)
    left = jnp.where(row >= col, one, other) / terms
    right = jnp.where(row < col, one, jnp.where(row == col, e[:, 0:1], other)) / docs - lean * lean_row
    eye = jnp.where(row == col, 1.0, 0.0).astype(F32)
    for m, gram in ((0, left), (1, right)):
        work[m, :, 0:K] = gram
        work[m, :, K : 2 * K] = eye
    factor(work)
    for m in range(2):
        inverse[m] = jnp.where(row >= col, work[m, :, K : 2 * K], 0.0)
    lean_out[...] = jnp.broadcast_to(lean, lean_out.shape)


def halves(x):
    hi = x.astype(BF16)
    return hi, (x - hi.astype(F32)).astype(BF16)


def mixed(lhs, rhs):
    return sum(jnp.dot(a, b, preferred_element_type=F32) for a, b in zip(lhs, rhs))


def bases(inverse, scaled, row_scale, gathered, lean, left_out, right_out):
    hi, low = halves(inverse[0])
    for b in range(0, RB, 2):
        pair = jnp.concatenate([scaled[b], scaled[b + 1]], axis=1)
        total = mixed((hi, low), (pair, pair))
        for u in range(2):
            basis = total[:, u * TILE : (u + 1) * TILE] / row_scale[b + u : b + u + 1, :]
            left_out[(b + u) * TILE : (b + u + 1) * TILE, :] = basis.T.astype(BF16)
    hi, low = halves(inverse[1])
    step = steps_of(gathered, 16)
    mean = lean[:, 0:1]
    for b in range(0, CB, 2):
        pair = jnp.concatenate(
            [wide(gathered[b + u, 0:K, :]) * step[:, b + u : b + u + 1] - mean for u in range(2)], axis=1
        )
        top, rest = halves(pair)
        total = mixed((hi, low, hi), (top, top, rest))
        for u in range(2):
            right_out[(b + u) * TILE : (b + u + 1) * TILE, :] = total[:, u * TILE : (u + 1) * TILE].T.astype(BF16)


def exchanged(x, axis):
    return lax.all_to_all(x, axis, split_axis=0, concat_axis=0, tiled=True)


def per_device(tile_values, tile_rows, tile_cols, tile_count, start_block):
    terms = float(RB * TILE * lax.axis_size(TERM))
    docs = float(CB * TILE * lax.axis_size(DOC))
    tiles = (tile_values, tile_rows, tile_cols, tile_count)
    vec = [((RB, 16, TILE), BF16), ((RB, 16, TILE), F32)]
    vector = ((16, RB, TILE), F32)
    scale = ((RB, TILE), F32)
    lists = pltpu.SMEM((1, CAP), jnp.int32)
    (part,) = call(
        first_rows,
        tiles,
        [vector],
        [*vec, (tile_values.shape, BF16), lists, lists, pltpu.SemaphoreType.DMA((2 + CAP // GROUP,))],
        [pl.BlockSpec(memory_space=pltpu.HBM)] * 3 + [SMEM],
        60,
    )
    part, _ = call(to_columns, (*tiles, exchanged(part, DOC)), [vector, scale], vec)
    (part,) = call(to_rows, (*tiles, exchanged(part, TERM), start_block), [((16, 24, TILE), F32)], vec)
    first = exchanged(part, DOC)
    part, row_scale = call(to_columns, (*tiles, first), [vector, scale], vec)
    part, col_scale = call(
        lambda *refs: left_product(docs, *refs),
        (*tiles, exchanged(part, TERM), first, start_block),
        [((RB, K, TILE), BF16), scale],
        [((CB, K + 16, TILE), BF16), ((RB, K + 16, TILE), F32)],
    )
    part, left_gram = call(
        left_rows, (exchanged(part, DOC), row_scale), [((16, K, TILE), BF16), ((K, K), F32)]
    )
    scaled = exchanged(part, DOC)
    half = (CB // 2, K + 16, TILE)
    keep, part = call(
        right_product,
        (*tiles, scaled, col_scale),
        [((CB // 2, K, TILE), F32), (half, jnp.int16)],
        [((CB, K, TILE), F32)],
    )
    part = lax.ppermute(part, "term_1", [(0, 1), (1, 0)])
    (part,) = call(core_sum, (keep, part), [(half, jnp.int16)], [((CB // 2, K, TILE), F32)])
    part, own = call(
        right_rows,
        (exchanged(part, "term_0"), left_gram),
        [((K, 3 * TILE), F32), ((K + 16, TILE), jnp.int16)],
    )
    gathered = lax.all_gather(own, TERM)
    part = exchanged(part.reshape(32, 8, 3 * TILE), PLANE)
    (part,) = call(sum_all, (part,), [((8, 8, 3 * TILE), F32)])
    (part,) = call(sum_all, (exchanged(part, "term_0"),), [((32, 8, 3 * TILE), F32)])
    grams = exchanged(part, PLANE).reshape(K, 3 * TILE)
    inverse, lean = call(
        lambda *refs: finish(terms, docs, *refs),
        (grams,),
        [((2, K, K), F32), ((K, TILE), F32)],
        [((2, K, 2 * K), F32)],
    )
    left_basis, right_basis = call(
        bases,
        (inverse, scaled, row_scale, gathered, lean),
        [((RB * TILE, K), BF16), ((CB * TILE, K), BF16)],
    )
    return (row_scale.reshape(-1), col_scale.reshape(-1), left_basis, right_basis)


def solution(mesh):
    torus = Mesh(mesh.devices.reshape(8, 2, 4, 4), ("term_0", "term_1", "doc_0", "doc_1"))
    placed = (P(TERM, DOC, None), P(TERM, DOC), P(TERM, DOC), P(TERM, DOC), P(DOC, None))
    return jax.shard_map(
        per_device,
        mesh=torus,
        in_specs=placed,
        out_specs=(P(TERM), P(DOC), P(TERM, None), P(DOC, None)),
        check_vma=False,
    )
```

```python
import jax
import jax.numpy as jnp
from jax import lax
from jax.experimental import pallas as pl
from jax.experimental.pallas import tpu as pltpu
from jax.sharding import Mesh
from jax.sharding import PartitionSpec as P

TILE = 128
K = 256
RB = 16
CB = 16
CAP = 48
GROUP = 24
PANEL = 64
TERM = ("term_0", "term_1")
DOC = ("doc_0", "doc_1")
F32 = jnp.float32
BF16 = jnp.bfloat16
PRECISE = lax.Precision.HIGHEST
VMEM = pl.BlockSpec(memory_space=pltpu.VMEM)
SMEM = pl.BlockSpec(memory_space=pltpu.SMEM)


def call(body, inputs, outs, scratch=(), specs=None, mib=16):
    return pl.pallas_call(
        body,
        out_shape=[jax.ShapeDtypeStruct(s, d) for s, d in outs],
        in_specs=specs or [SMEM if a.dtype == jnp.int32 else VMEM for a in inputs],
        out_specs=[VMEM] * len(outs),
        scratch_shapes=[pltpu.VMEM(s[0], s[1]) if isinstance(s, tuple) else s for s in scratch],
        compiler_params=pltpu.CompilerParams(vmem_limit_bytes=int(mib * 1024 * 1024)),
    )(*inputs)


def thirds(x):
    hi = x.astype(BF16)
    rest = x - hi.astype(F32)
    mid = rest.astype(BF16)
    low = (rest - mid.astype(F32)).astype(BF16)
    return hi, mid, low


def put_thirds(ref, vec, base):
    hi, mid, low = thirds(vec)
    row = lax.broadcasted_iota(jnp.int32, (16, TILE), 0)
    for b in range(RB):
        parts = [jnp.broadcast_to(p[b : b + 1].astype(F32), (16, TILE)) for p in (hi, mid, low)]
        rows = jnp.where(row == 0, parts[0], jnp.where(row == 1, parts[1], jnp.where(row == 2, parts[2], 0.0)))
        ref[b, base : base + 16, :] = rows.astype(BF16)


def over_tiles(count, values, source, target, src_ref, acc_ref, transposed, group, ready=None):
    acc_ref[...] = jnp.zeros(acc_ref.shape, F32)
    dims = (((1,), (1,)), ((), ())) if transposed else (((1,), (0,)), ((), ()))

    def visit(g, _):
        products = []
        for u in range(group):
            s = g * group + u
            tile = values[s]
            tile = jnp.where(s < count, tile, jnp.zeros_like(tile))
            products.append(
                lax.dot_general(src_ref[source[0, s]], tile, dims, preferred_element_type=F32)
            )
        for u in range(group):
            s = g * group + u
            acc_ref[target[0, s]] += products[u]
        return 0

    if ready is None and group < CAP:
        lax.fori_loop(0, (count + group - 1) // group, visit, 0)
        return
    for g in range(CAP // group):
        if ready is not None:
            ready(g)
        visit(g, 0)


def send_vector(out_ref, acc_ref):
    vec = jnp.sum(acc_ref[...], axis=1)
    for i in range(16):
        out_ref[i, 0:RB, :] = vec


def first_rows(values_in, rows_in, cols_in, count, out, src, acc, values, rows, cols, sems):
    parts = CAP // GROUP
    copies = [pltpu.make_async_copy(rows_in, rows, sems.at[0]), pltpu.make_async_copy(cols_in, cols, sems.at[1])]
    for g in range(parts):
        own = pl.ds(g * GROUP, GROUP)
        copies.append(pltpu.make_async_copy(values_in.at[own], values.at[own], sems.at[2 + g]))
    for copy in copies:
        copy.start()
    put_thirds(src, jnp.ones((CB, TILE), F32), 0)
    copies[0].wait()
    copies[1].wait()
    over_tiles(count[0, 0], values, cols, rows, src, acc, True, GROUP, lambda g: copies[2 + g].wait())
    send_vector(out, acc)


def to_columns(values, rows, cols, count, got, out, scale, src, acc):
    vec = 1.0 / jnp.sum(got[...], axis=0)[0:RB]
    scale[...] = vec
    put_thirds(src, vec, 0)
    over_tiles(count[0, 0], values, rows, cols, src, acc, False, CAP)
    send_vector(out, acc)


def to_rows(values, rows, cols, count, got, start, out, src, acc):
    put_thirds(src, 1.0 / jnp.sum(got[...], axis=0), 0)
    over_tiles(count[0, 0], values, cols, rows, src, acc, True, GROUP)
    send_vector(out, acc)
    mean = jnp.sum(start[...].astype(F32), axis=0, keepdims=True)
    for i in range(16):
        out[i, 16:17, :] = mean[:, :TILE]
        out[i, 17:18, :] = mean[:, TILE:]
        out[i, 18:24, :] = jnp.zeros((6, TILE), F32)


def left_product(docs, values, rows, cols, count, got, first, start, out, scale, src, acc):
    vec = 1.0 / jnp.sum(got[...], axis=0)
    scale[...] = vec
    put_thirds(src, vec, K)
    for b in range(CB):
        block = start[b * TILE : (b + 1) * TILE, :].T.astype(F32)
        src[b, 0:K, :] = (block * vec[b : b + 1, :]).astype(BF16)
    mean = jnp.sum(first[...], axis=0)[16:18] / docs
    mean = jnp.concatenate([jnp.broadcast_to(mean[h : h + 1], (TILE, TILE)).T for h in range(2)], axis=0)
    over_tiles(count[0, 0], values, cols, rows, src, acc, True, GROUP)
    for b in range(RB):
        weight = jnp.sum(acc[b, K : K + 16, :], axis=0, keepdims=True)
        out[b] = (acc[b, 0:K, :] - mean * weight).astype(out.dtype)


def left_rows(got, row_scale, out, gram):
    d = lax.axis_index(DOC)
    scale = row_scale[pl.ds(d, 1), :]
    left = scale * jnp.sum(got[...].astype(F32), axis=0)
    sent = (left * scale).astype(BF16)
    for i in range(16):
        out[i] = sent
    gram[...] = lax.dot_general(left, left, (((1,), (1,)), ((), ())), precision=PRECISE, preferred_element_type=F32)


LEVELS = 32000.0
STEPS = 64.0


def code_of(peak):
    return jnp.ceil(jnp.log2(jnp.maximum(peak, 1e-37)) * STEPS)


def code_lines(code):
    lines = jnp.broadcast_to(code, (K, TILE)).T
    return jnp.concatenate([lines[0:8, :TILE], lines[0:8, TILE:]], axis=0).astype(jnp.int32).astype(jnp.int16)


def counted(x, code):
    steps = x * (jnp.exp2(code * (-1.0 / STEPS)) * LEVELS)
    return jnp.floor(steps + 0.5).astype(jnp.int32).astype(jnp.int16)


def wide(x):
    return x.astype(jnp.int32).astype(F32)


def steps_of(got, count):
    lines = [wide(got[i, K : K + 16, :]) for i in range(count)]
    code = jnp.concatenate(
        [jnp.concatenate([x[h : h + 1] for x in lines], axis=0) for h in (0, 8)], axis=1
    ).T
    return jnp.exp2(code * (1.0 / STEPS)) * (1.0 / LEVELS)


def right_product(values, rows, cols, count, scaled, col_scale, keep, send, acc):
    over_tiles(count[0, 0], values, rows, cols, scaled, acc, False, GROUP)
    core = lax.axis_index("term_1")
    peak = jnp.zeros((K, TILE), F32)
    for i in range(CB // 2):
        mine, its = 2 * i + core, 2 * i + 1 - core
        keep[i] = acc[mine] * col_scale[pl.ds(mine, 1), :]
        part = acc[its] * col_scale[pl.ds(its, 1), :]
        acc[its] = part
        peak = jnp.maximum(peak, jnp.abs(part))
    code = code_of(jnp.max(peak, axis=1, keepdims=True))
    lines = code_lines(code)
    for i in range(CB // 2):
        send[i, 0:K, :] = counted(acc[2 * i + 1 - core], code)
        send[i, K : K + 16, :] = lines


def core_sum(keep, got, out, total):
    step = steps_of(got, 8)[:, 0:1]
    peak = jnp.zeros((K, TILE), F32)
    for i in range(CB // 2):
        part = keep[i] + wide(got[i, 0:K, :]) * step
        total[i] = part
        peak = jnp.maximum(peak, jnp.abs(part))
    code = code_of(jnp.max(peak, axis=1, keepdims=True))
    lines = code_lines(code)
    for i in range(CB // 2):
        out[i, 0:K, :] = counted(total[i], code)
        out[i, K : K + 16, :] = lines


def iotas(shape=(K, K)):
    return lax.broadcasted_iota(jnp.int32, shape, 0), lax.broadcasted_iota(jnp.int32, shape, 1)


def right_rows(got, left_gram, out, own):
    step = steps_of(got, 8)
    right = wide(got[0, 0:K, :]) * step[:, 0:1]
    for i in range(1, 8):
        right += wide(got[i, 0:K, :]) * step[:, i : i + 1]
    code = code_of(jnp.max(jnp.abs(right), axis=1, keepdims=True))
    own[0:K, :] = counted(right, code)
    own[K : K + 16, :] = code_lines(code)
    gram = lax.dot_general(right, right, (((1,), (1,)), ((), ())), precision=PRECISE, preferred_element_type=F32)
    row, col = iotas()
    packed = jnp.where(row >= col, left_gram[...], gram)
    diag = jnp.sum(jnp.where(row == col, gram, 0.0), axis=1, keepdims=True)
    lean = jnp.sum(right, axis=1, keepdims=True)
    lane = lax.broadcasted_iota(jnp.int32, (K, TILE), 1)
    extra = jnp.where(lane == 0, diag, jnp.where(lane == 1, lean, 0.0))
    out[:, 0:K] = packed
    out[:, K : K + TILE] = extra


FINE = 64000.0
OWN = K + 16
MID = OWN + 48
LOW = MID + 48


def sum_docs(got, own, out):
    out[0:OWN, :] = own[...]
    total = jnp.sum(got[...], axis=0)
    code = code_of(jnp.max(jnp.abs(total), axis=1, keepdims=True))
    steps = total * (jnp.exp2(code * (-1.0 / STEPS)) * LEVELS)
    whole = jnp.floor(steps + 0.5)
    part = jnp.floor((steps - whole) * FINE + 0.5)
    for h in range(3):
        lanes = slice(h * TILE, (h + 1) * TILE)
        out[OWN + 16 * h : OWN + 16 * h + 16, :] = whole[:, lanes].astype(jnp.int32).astype(jnp.int16)
        out[MID + 16 * h : MID + 16 * h + 16, :] = part[:, lanes].astype(jnp.int32).astype(jnp.int16)
    out[LOW : LOW + 16, :] = jnp.broadcast_to(code, (16, TILE)).astype(jnp.int32).astype(jnp.int16)


def sum_terms(got, out):
    total = [jnp.zeros((16, TILE), F32)] * 3
    for i in range(16):
        step = jnp.exp2(wide(got[i, LOW : LOW + 16, :]) * (1.0 / STEPS)) * (1.0 / LEVELS)
        for h in range(3):
            whole = wide(got[i, OWN + 16 * h : OWN + 16 * h + 16, :])
            part = wide(got[i, MID + 16 * h : MID + 16 * h + 16, :])
            total[h] = total[h] + (whole + part * (1.0 / FINE)) * step
    total = jnp.concatenate(total, axis=1)
    for i in range(16):
        out[i] = total


def spread(x, lane):
    return jnp.broadcast_to(x[:, :, lane : lane + 1], x.shape)


def eliminate(blocks, at):
    blocks = list(blocks)
    sub = lax.broadcasted_iota(jnp.int32, (2, 8, TILE), 1)
    for g in range(len(blocks)):
        lead = blocks[g]
        lanes = [at + 8 * g + b for b in range(8)]
        head = [spread(lead, l) for l in lanes]
        pivots = jnp.ones((2, 8, TILE), F32)
        lines, inverses, entries = [], [], []
        for a in range(8):
            pivot = head[a][:, a : a + 1]
            inv = 1.0 / pivot
            line = lead[:, a : a + 1]
            entry = [head[b][:, a : a + 1] for b in range(8)]
            lines.append(line)
            inverses.append(inv)
            entries.append(entry)
            pivots = jnp.where(sub == a, pivot, pivots)
            f = jnp.where(sub > a, head[a] * inv, 0.0)
            lead = lead - f * line
            for b in range(a + 1, 8):
                head[b] = head[b] - f * entry[b]
        for j in range(g + 1, len(blocks)):
            cols = [spread(blocks[j], l) for l in lanes]
            total = blocks[j]
            for a in range(8):
                f = cols[a] * inverses[a]
                total = total - f * lines[a]
                for b in range(a + 1, 8):
                    cols[b] = cols[b] - f * entries[a][b]
            blocks[j] = total
        blocks[g] = lead * lax.rsqrt(pivots)
    return blocks


def precise(lhs, rhs, contract=1):
    return lax.dot_general(lhs, rhs, (((contract,), (0,)), ((), ())), precision=PRECISE, preferred_element_type=F32)


def factor(work):
    lane = lax.broadcasted_iota(jnp.int32, (2, PANEL, TILE), 2)
    line = lax.broadcasted_iota(jnp.int32, (2, PANEL, TILE), 1)
    own = work[:, 0:PANEL, 0:TILE]
    for start in range(0, K, PANEL):
        first = (start // TILE) * TILE
        span = slice(first, first + 3 * TILE)
        end = start + PANEL
        at = start - first
        other = PANEL - at
        unit = jnp.where(lane == line + other, 1.0, 0.0)
        here = (lane >= at) & (lane < at + PANEL)
        block = jnp.where(here, own, unit)
        done = jnp.concatenate(eliminate([block[:, 8 * j : 8 * j + 8] for j in range(PANEL // 8)], at), axis=1)
        inverses = [done[m, :, other : other + PANEL] for m in range(2)]
        if end < K:
            then = (end // TILE) * TILE
            ahead = []
            for m in range(2):
                upper = precise(inverses[m], work[m, start:end, then : then + TILE])
                cut = upper[:, end - then : end - then + PANEL]
                ahead.append(work[m, end : end + PANEL, then : then + TILE] - precise(cut, upper, 0))
            own = jnp.stack(ahead)
        for m in range(2):
            panel = precise(inverses[m], work[m, start:end, span])
            work[m, start:end, span] = panel
            if end < K:
                work[m, end:K, span] -= precise(panel[:, end - first : K - first], panel, 0)


def finish(terms, docs, grams, inverse, lean_out, work):
    row, col = iotas()
    one = grams[:, 0:K]
    other = one.T
    e = grams[:, K : K + TILE]
    lean = e[:, 1:2] / docs
    lean_row = jnp.sum(jnp.where(row == col, lean, 0.0), axis=0, keepdims=True)
    left = jnp.where(row >= col, one, other) / terms
    right = jnp.where(row < col, one, jnp.where(row == col, e[:, 0:1], other)) / docs - lean * lean_row
    eye = jnp.where(row == col, 1.0, 0.0).astype(F32)
    for m, gram in ((0, left), (1, right)):
        work[m, :, 0:K] = gram
        work[m, :, K : 2 * K] = eye
    factor(work)
    for m in range(2):
        inverse[m] = jnp.where(row >= col, work[m, :, K : 2 * K], 0.0)
    lean_out[...] = jnp.broadcast_to(lean, lean_out.shape)


def halves(x):
    hi = x.astype(BF16)
    return hi, (x - hi.astype(F32)).astype(BF16)


def mixed(lhs, rhs):
    return sum(jnp.dot(a, b, preferred_element_type=F32) for a, b in zip(lhs, rhs))


def bases(inverse, scaled, row_scale, gathered, lean, left_out, right_out):
    hi, low = halves(inverse[0])
    for b in range(0, RB, 2):
        pair = jnp.concatenate([scaled[b], scaled[b + 1]], axis=1)
        total = mixed((hi, low), (pair, pair))
        for u in range(2):
            basis = total[:, u * TILE : (u + 1) * TILE] / row_scale[b + u : b + u + 1, :]
            left_out[(b + u) * TILE : (b + u + 1) * TILE, :] = basis.T.astype(BF16)
    hi, low = halves(inverse[1])
    step = steps_of(gathered, 16)
    mean = lean[:, 0:1]
    for b in range(0, CB, 2):
        pair = jnp.concatenate(
            [wide(gathered[b + u, 0:K, :]) * step[:, b + u : b + u + 1] - mean for u in range(2)], axis=1
        )
        top, rest = halves(pair)
        total = mixed((hi, low, hi), (top, top, rest))
        for u in range(2):
            right_out[(b + u) * TILE : (b + u + 1) * TILE, :] = total[:, u * TILE : (u + 1) * TILE].T.astype(BF16)


def exchanged(x, axis):
    return lax.all_to_all(x, axis, split_axis=0, concat_axis=0, tiled=True)


def per_device(tile_values, tile_rows, tile_cols, tile_count, start_block):
    terms = float(RB * TILE * lax.axis_size(TERM))
    docs = float(CB * TILE * lax.axis_size(DOC))
    tiles = (tile_values, tile_rows, tile_cols, tile_count)
    vec = [((RB, 16, TILE), BF16), ((RB, 16, TILE), F32)]
    vector = ((16, RB, TILE), F32)
    scale = ((RB, TILE), F32)
    lists = pltpu.SMEM((1, CAP), jnp.int32)
    (part,) = call(
        first_rows,
        tiles,
        [vector],
        [*vec, (tile_values.shape, BF16), lists, lists, pltpu.SemaphoreType.DMA((2 + CAP // GROUP,))],
        [pl.BlockSpec(memory_space=pltpu.HBM)] * 3 + [SMEM],
        60,
    )
    part, _ = call(to_columns, (*tiles, exchanged(part, DOC)), [vector, scale], vec)
    (part,) = call(to_rows, (*tiles, exchanged(part, TERM), start_block), [((16, 24, TILE), F32)], vec)
    first = exchanged(part, DOC)
    part, row_scale = call(to_columns, (*tiles, first), [vector, scale], vec)
    part, col_scale = call(
        lambda *refs: left_product(docs, *refs),
        (*tiles, exchanged(part, TERM), first, start_block),
        [((RB, K, TILE), BF16), scale],
        [((CB, K + 16, TILE), BF16), ((RB, K + 16, TILE), F32)],
    )
    part, left_gram = call(
        left_rows, (exchanged(part, DOC), row_scale), [((16, K, TILE), BF16), ((K, K), F32)]
    )
    scaled = exchanged(part, DOC)
    half = (CB // 2, K + 16, TILE)
    keep, part = call(
        right_product,
        (*tiles, scaled, col_scale),
        [((CB // 2, K, TILE), F32), (half, jnp.int16)],
        [((CB, K, TILE), F32)],
    )
    part = lax.ppermute(part, "term_1", [(0, 1), (1, 0)])
    (part,) = call(core_sum, (keep, part), [(half, jnp.int16)], [((CB // 2, K, TILE), F32)])
    part, own = call(
        right_rows,
        (exchanged(part, "term_0"), left_gram),
        [((K, 3 * TILE), F32), ((K + 16, TILE), jnp.int16)],
    )
    part = exchanged(part.reshape(16, 16, 3 * TILE), DOC)
    (part,) = call(sum_docs, (part, own), [((LOW + 16, TILE), jnp.int16)])
    gathered = lax.all_gather(part, TERM)
    (part,) = call(sum_terms, (gathered,), [((16, 16, 3 * TILE), F32)])
    grams = exchanged(part, DOC).reshape(K, 3 * TILE)
    inverse, lean = call(
        lambda *refs: finish(terms, docs, *refs),
        (grams,),
        [((2, K, K), F32), ((K, TILE), F32)],
        [((2, K, 2 * K), F32)],
    )
    left_basis, right_basis = call(
        bases,
        (inverse, scaled, row_scale, gathered, lean),
        [((RB * TILE, K), BF16), ((CB * TILE, K), BF16)],
    )
    return (row_scale.reshape(-1), col_scale.reshape(-1), left_basis, right_basis)


def solution(mesh):
    torus = Mesh(mesh.devices.reshape(8, 2, 4, 4), ("term_0", "term_1", "doc_0", "doc_1"))
    placed = (P(TERM, DOC, None), P(TERM, DOC), P(TERM, DOC), P(TERM, DOC), P(DOC, None))
    return jax.shard_map(
        per_device,
        mesh=torus,
        in_specs=placed,
        out_specs=(P(TERM), P(DOC), P(TERM, None), P(DOC, None)),
        check_vma=False,
    )
```

```python
import jax
import jax.numpy as jnp
from jax import lax
from jax.experimental import pallas as pl
from jax.experimental.pallas import tpu as pltpu
from jax.sharding import Mesh
from jax.sharding import PartitionSpec as P

TILE = 128
K = 256
RB = 16
CB = 16
CAP = 48
GROUP = 24
PANEL = 64
TERM = ("term_0", "term_1")
DOC = ("doc_0", "doc_1")
F32 = jnp.float32
BF16 = jnp.bfloat16
PRECISE = lax.Precision.HIGHEST
VMEM = pl.BlockSpec(memory_space=pltpu.VMEM)
SMEM = pl.BlockSpec(memory_space=pltpu.SMEM)


def call(body, inputs, outs, scratch=(), specs=None, mib=16, out_specs=None):
    return pl.pallas_call(
        body,
        out_shape=[jax.ShapeDtypeStruct(s, d) for s, d in outs],
        in_specs=specs or [SMEM if a.dtype == jnp.int32 else VMEM for a in inputs],
        out_specs=out_specs or [VMEM] * len(outs),
        scratch_shapes=[pltpu.VMEM(s[0], s[1]) if isinstance(s, tuple) else s for s in scratch],
        compiler_params=pltpu.CompilerParams(vmem_limit_bytes=int(mib * 1024 * 1024)),
    )(*inputs)


def thirds(x):
    hi = x.astype(BF16)
    rest = x - hi.astype(F32)
    mid = rest.astype(BF16)
    low = (rest - mid.astype(F32)).astype(BF16)
    return hi, mid, low


def put_thirds(ref, vec, base):
    hi, mid, low = thirds(vec)
    row = lax.broadcasted_iota(jnp.int32, (16, TILE), 0)
    for b in range(RB):
        parts = [jnp.broadcast_to(p[b : b + 1].astype(F32), (16, TILE)) for p in (hi, mid, low)]
        rows = jnp.where(row == 0, parts[0], jnp.where(row == 1, parts[1], jnp.where(row == 2, parts[2], 0.0)))
        ref[b, base : base + 16, :] = rows.astype(BF16)


def over_tiles(count, values, source, target, src_ref, acc_ref, transposed, group, ready=None):
    acc_ref[...] = jnp.zeros(acc_ref.shape, F32)
    dims = (((1,), (1,)), ((), ())) if transposed else (((1,), (0,)), ((), ()))

    def visit(g, _):
        products = []
        for u in range(group):
            s = g * group + u
            tile = values[s]
            tile = jnp.where(s < count, tile, jnp.zeros_like(tile))
            products.append(
                lax.dot_general(src_ref[source[0, s]], tile, dims, preferred_element_type=F32)
            )
        for u in range(group):
            s = g * group + u
            acc_ref[target[0, s]] += products[u]
        return 0

    if ready is None and group < CAP:
        lax.fori_loop(0, (count + group - 1) // group, visit, 0)
        return
    for g in range(CAP // group):
        if ready is not None:
            ready(g)
        visit(g, 0)


def send_vector(out_ref, acc_ref):
    vec = jnp.sum(acc_ref[...], axis=1)
    for i in range(16):
        out_ref[i, 0:RB, :] = vec


def first_rows(values_in, rows_in, cols_in, count, out, src, acc, values, rows, cols, sems):
    parts = CAP // GROUP
    copies = [pltpu.make_async_copy(rows_in, rows, sems.at[0]), pltpu.make_async_copy(cols_in, cols, sems.at[1])]
    for g in range(parts):
        own = pl.ds(g * GROUP, GROUP)
        copies.append(pltpu.make_async_copy(values_in.at[own], values.at[own], sems.at[2 + g]))
    for copy in copies:
        copy.start()
    put_thirds(src, jnp.ones((CB, TILE), F32), 0)
    copies[0].wait()
    copies[1].wait()
    over_tiles(count[0, 0], values, cols, rows, src, acc, True, GROUP, lambda g: copies[2 + g].wait())
    send_vector(out, acc)


def to_columns(values, rows, cols, count, got, out, scale, src, acc):
    vec = 1.0 / jnp.sum(got[...], axis=0)[0:RB]
    scale[...] = vec
    put_thirds(src, vec, 0)
    over_tiles(count[0, 0], values, rows, cols, src, acc, False, CAP)
    send_vector(out, acc)


def to_rows(values, rows, cols, count, got, start, out, src, acc):
    put_thirds(src, 1.0 / jnp.sum(got[...], axis=0), 0)
    over_tiles(count[0, 0], values, cols, rows, src, acc, True, GROUP)
    send_vector(out, acc)
    mean = jnp.sum(start[...].astype(F32), axis=0, keepdims=True)
    for i in range(16):
        out[i, 16:17, :] = mean[:, :TILE]
        out[i, 17:18, :] = mean[:, TILE:]
        out[i, 18:24, :] = jnp.zeros((6, TILE), F32)


def left_product(docs, values, rows, cols, count, got, first, start, out, scale, src, acc):
    vec = 1.0 / jnp.sum(got[...], axis=0)
    scale[...] = vec
    put_thirds(src, vec, K)
    for b in range(CB):
        block = start[b * TILE : (b + 1) * TILE, :].T.astype(F32)
        src[b, 0:K, :] = (block * vec[b : b + 1, :]).astype(BF16)
    mean = jnp.sum(first[...], axis=0)[16:18] / docs
    mean = jnp.concatenate([jnp.broadcast_to(mean[h : h + 1], (TILE, TILE)).T for h in range(2)], axis=0)
    over_tiles(count[0, 0], values, cols, rows, src, acc, True, CAP)
    for b in range(RB):
        weight = jnp.sum(acc[b, K : K + 16, :], axis=0, keepdims=True)
        out[b] = (acc[b, 0:K, :] - mean * weight).astype(out.dtype)


def left_rows(got, row_scale, out, gram):
    d = lax.axis_index(DOC)
    scale = row_scale[pl.ds(d, 1), :]
    left = scale * jnp.sum(got[...].astype(F32), axis=0)
    sent = (left * scale).astype(BF16)
    for i in range(16):
        out[i] = sent
    gram[...] = lax.dot_general(left, left, (((1,), (1,)), ((), ())), precision=PRECISE, preferred_element_type=F32)


LEVELS = 32000.0
STEPS = 64.0


def code_of(peak):
    return jnp.ceil(jnp.log2(jnp.maximum(peak, 1e-37)) * STEPS)


def code_lines(code):
    lines = jnp.broadcast_to(code, (K, TILE)).T
    return jnp.concatenate([lines[0:8, :TILE], lines[0:8, TILE:]], axis=0).astype(jnp.int32).astype(jnp.int16)


def counted(x, code):
    steps = x * (jnp.exp2(code * (-1.0 / STEPS)) * LEVELS)
    return jnp.floor(steps + 0.5).astype(jnp.int32).astype(jnp.int16)


def wide(x):
    return x.astype(jnp.int32).astype(F32)


def steps_of(got, count):
    lines = [wide(got[i, K : K + 16, :]) for i in range(count)]
    code = jnp.concatenate(
        [jnp.concatenate([x[h : h + 1] for x in lines], axis=0) for h in (0, 8)], axis=1
    ).T
    return jnp.exp2(code * (1.0 / STEPS)) * (1.0 / LEVELS)


def right_product(values, rows, cols, count, scaled, col_scale, keep, send, acc):
    over_tiles(count[0, 0], values, rows, cols, scaled, acc, False, CAP)
    core = lax.axis_index("term_1")
    peak = jnp.zeros((K, TILE), F32)
    for i in range(CB // 2):
        mine, its = 2 * i + core, 2 * i + 1 - core
        keep[i] = acc[mine] * col_scale[pl.ds(mine, 1), :]
        part = acc[its] * col_scale[pl.ds(its, 1), :]
        acc[its] = part
        peak = jnp.maximum(peak, jnp.abs(part))
    code = code_of(jnp.max(peak, axis=1, keepdims=True))
    lines = code_lines(code)
    for i in range(CB // 2):
        send[i, 0:K, :] = counted(acc[2 * i + 1 - core], code)
        send[i, K : K + 16, :] = lines


def core_sum(keep, got, out, total):
    step = steps_of(got, 8)[:, 0:1]
    peak = jnp.zeros((K, TILE), F32)
    for i in range(CB // 2):
        part = keep[i] + wide(got[i, 0:K, :]) * step
        total[i] = part
        peak = jnp.maximum(peak, jnp.abs(part))
    code = code_of(jnp.max(peak, axis=1, keepdims=True))
    lines = code_lines(code)
    for i in range(CB // 2):
        out[i, 0:K, :] = counted(total[i], code)
        out[i, K : K + 16, :] = lines


def iotas(shape=(K, K)):
    return lax.broadcasted_iota(jnp.int32, shape, 0), lax.broadcasted_iota(jnp.int32, shape, 1)


def right_rows(got, left_gram, out, own):
    step = steps_of(got, 8)
    right = wide(got[0, 0:K, :]) * step[:, 0:1]
    for i in range(1, 8):
        right += wide(got[i, 0:K, :]) * step[:, i : i + 1]
    code = code_of(jnp.max(jnp.abs(right), axis=1, keepdims=True))
    own[0:K, :] = counted(right, code)
    own[K : K + 16, :] = code_lines(code)
    gram = lax.dot_general(right, right, (((1,), (1,)), ((), ())), precision=PRECISE, preferred_element_type=F32)
    row, col = iotas()
    packed = jnp.where(row >= col, left_gram[...], gram)
    diag = jnp.sum(jnp.where(row == col, gram, 0.0), axis=1, keepdims=True)
    lean = jnp.sum(right, axis=1, keepdims=True)
    lane = lax.broadcasted_iota(jnp.int32, (K, TILE), 1)
    extra = jnp.where(lane == 0, diag, jnp.where(lane == 1, lean, 0.0))
    out[:, 0:K] = packed
    out[:, K : K + TILE] = extra


FINE = 64000.0
OWN = K + 16
MID = OWN + 48
LOW = MID + 48


def sum_docs(got, own, out):
    out[0:OWN, :] = own[...]
    total = jnp.sum(got[...], axis=0)
    code = code_of(jnp.max(jnp.abs(total), axis=1, keepdims=True))
    steps = total * (jnp.exp2(code * (-1.0 / STEPS)) * LEVELS)
    whole = jnp.floor(steps + 0.5)
    part = jnp.floor((steps - whole) * FINE + 0.5)
    for h in range(3):
        lanes = slice(h * TILE, (h + 1) * TILE)
        out[OWN + 16 * h : OWN + 16 * h + 16, :] = whole[:, lanes].astype(jnp.int32).astype(jnp.int16)
        out[MID + 16 * h : MID + 16 * h + 16, :] = part[:, lanes].astype(jnp.int32).astype(jnp.int16)
    out[LOW : LOW + 16, :] = jnp.broadcast_to(code, (16, TILE)).astype(jnp.int32).astype(jnp.int16)


def sum_terms(got, out):
    total = [jnp.zeros((16, TILE), F32)] * 3
    for i in range(16):
        step = jnp.exp2(wide(got[i, LOW : LOW + 16, :]) * (1.0 / STEPS)) * (1.0 / LEVELS)
        for h in range(3):
            whole = wide(got[i, OWN + 16 * h : OWN + 16 * h + 16, :])
            part = wide(got[i, MID + 16 * h : MID + 16 * h + 16, :])
            total[h] = total[h] + (whole + part * (1.0 / FINE)) * step
    total = jnp.concatenate(total, axis=1)
    for i in range(16):
        out[i] = total


def spread(x, lane):
    return jnp.broadcast_to(x[:, :, lane : lane + 1], x.shape)


def eliminate(blocks, at):
    blocks = [list(b) for b in blocks]
    sub = lax.broadcasted_iota(jnp.int32, (2, 8, TILE), 1)
    for g in range(len(blocks)):
        lead = blocks[g]
        lanes = [at + 8 * g + b for b in range(8)]
        head = [spread(lead[0], l) for l in lanes]
        pivots = jnp.ones((2, 8, TILE), F32)
        lines, inverses, entries = [], [], []
        for a in range(8):
            pivot = head[a][:, a : a + 1]
            inv = 1.0 / pivot
            line = [x[:, a : a + 1] for x in lead]
            entry = [head[b][:, a : a + 1] for b in range(8)]
            lines.append(line)
            inverses.append(inv)
            entries.append(entry)
            pivots = jnp.where(sub == a, pivot, pivots)
            f = jnp.where(sub > a, head[a], 0.0) * inv
            lead = [x - f * y for x, y in zip(lead, line)]
            for b in range(a + 1, 8):
                head[b] = head[b] - f * entry[b]
        for j in range(g + 1, len(blocks)):
            cols = [spread(blocks[j][0], l) for l in lanes]
            total = blocks[j]
            for a in range(8):
                f = cols[a] * inverses[a]
                total = [x - f * y for x, y in zip(total, lines[a])]
                for b in range(a + 1, 8):
                    cols[b] = cols[b] - f * entries[a][b]
            blocks[j] = total
        root = lax.rsqrt(pivots)
        blocks[g] = [x * root for x in lead]
    return blocks


def precise(lhs, rhs, contract=1):
    return lax.dot_general(lhs, rhs, (((contract,), (0,)), ((), ())), precision=PRECISE, preferred_element_type=F32)


def factor(work):
    lane = lax.broadcasted_iota(jnp.int32, (2, PANEL, TILE), 2)
    line = lax.broadcasted_iota(jnp.int32, (2, PANEL, TILE), 1)
    own = work[:, 0:PANEL, 0:TILE]
    for start in range(0, K, PANEL):
        first = (start // TILE) * TILE
        span = slice(first, first + 3 * TILE)
        end = start + PANEL
        at = start - first
        other = PANEL - at
        unit = jnp.where(lane == line + other, 1.0, 0.0)
        here = (lane >= at) & (lane < at + PANEL)
        parts = [jnp.where(here, own, unit)]
        then = (end // TILE) * TILE
        if end < K:
            parts.append(own if then == first else work[:, start:end, then : then + TILE])
        done = eliminate([[x[:, 8 * j : 8 * j + 8] for x in parts] for j in range(PANEL // 8)], at)
        done = [jnp.concatenate([b[i] for b in done], axis=1) for i in range(len(parts))]
        inverses = [done[0][m, :, other : other + PANEL] for m in range(2)]
        if end < K:
            ahead = []
            for m in range(2):
                upper = done[1][m]
                cut = upper[:, end - then : end - then + PANEL]
                ahead.append(work[m, end : end + PANEL, then : then + TILE] - precise(cut, upper, 0))
            own = jnp.stack(ahead)
        for m in range(2):
            panel = precise(inverses[m], work[m, start:end, span])
            work[m, start:end, span] = panel
            if end < K:
                work[m, end:K, span] -= precise(panel[:, end - first : K - first], panel, 0)


def finish(terms, docs, grams, inverse, lean_out, work):
    row, col = iotas()
    one = grams[:, 0:K]
    other = one.T
    e = grams[:, K : K + TILE]
    lean = e[:, 1:2] / docs
    lean_row = jnp.sum(jnp.where(row == col, lean, 0.0), axis=0, keepdims=True)
    left = jnp.where(row >= col, one, other) / terms
    right = jnp.where(row < col, one, jnp.where(row == col, e[:, 0:1], other)) / docs - lean * lean_row
    eye = jnp.where(row == col, 1.0, 0.0).astype(F32)
    for m, gram in ((0, left), (1, right)):
        work[m, :, 0:K] = gram
        work[m, :, K : 2 * K] = eye
    factor(work)
    for m in range(2):
        inverse[m] = jnp.where(row >= col, work[m, :, K : 2 * K], 0.0)
    lean_out[...] = jnp.broadcast_to(lean, lean_out.shape)


def halves(x):
    hi = x.astype(BF16)
    return hi, (x - hi.astype(F32)).astype(BF16)


def mixed(lhs, rhs):
    return sum(jnp.dot(a, b, preferred_element_type=F32) for a, b in zip(lhs, rhs))


def bases(inverse, scaled, row_scale, gathered, lean, left_out, right_out, left_held, right_held, sems):
    copies = []

    def send(rows, out, b):
        own = pl.ds(b * TILE, 2 * TILE)
        copies.append(pltpu.make_async_copy(rows.at[own], out.at[own], sems.at[len(copies)]))
        copies[-1].start()

    hi, low = halves(inverse[0])
    for b in range(0, RB, 2):
        pair = jnp.concatenate([scaled[b], scaled[b + 1]], axis=1)
        total = mixed((hi, low), (pair, pair))
        for u in range(2):
            basis = total[:, u * TILE : (u + 1) * TILE] / row_scale[b + u : b + u + 1, :]
            left_held[(b + u) * TILE : (b + u + 1) * TILE, :] = basis.T.astype(BF16)
        send(left_held, left_out, b)
    hi, low = halves(inverse[1])
    step = steps_of(gathered, 16)
    mean = lean[:, 0:1]
    for b in range(0, CB, 2):
        pair = jnp.concatenate(
            [wide(gathered[b + u, 0:K, :]) * step[:, b + u : b + u + 1] - mean for u in range(2)], axis=1
        )
        top, rest = halves(pair)
        total = mixed((hi, low, hi), (top, top, rest))
        for u in range(2):
            right_held[(b + u) * TILE : (b + u + 1) * TILE, :] = total[:, u * TILE : (u + 1) * TILE].T.astype(BF16)
        send(right_held, right_out, b)
    for copy in copies:
        copy.wait()


def exchanged(x, axis):
    return lax.all_to_all(x, axis, split_axis=0, concat_axis=0, tiled=True)


def per_device(tile_values, tile_rows, tile_cols, tile_count, start_block):
    terms = float(RB * TILE * lax.axis_size(TERM))
    docs = float(CB * TILE * lax.axis_size(DOC))
    tiles = (tile_values, tile_rows, tile_cols, tile_count)
    vec = [((RB, 16, TILE), BF16), ((RB, 16, TILE), F32)]
    vector = ((16, RB, TILE), F32)
    scale = ((RB, TILE), F32)
    lists = pltpu.SMEM((1, CAP), jnp.int32)
    (part,) = call(
        first_rows,
        tiles,
        [vector],
        [*vec, (tile_values.shape, BF16), lists, lists, pltpu.SemaphoreType.DMA((2 + CAP // GROUP,))],
        [pl.BlockSpec(memory_space=pltpu.HBM)] * 3 + [SMEM],
        60,
    )
    part, _ = call(to_columns, (*tiles, exchanged(part, DOC)), [vector, scale], vec)
    (part,) = call(to_rows, (*tiles, exchanged(part, TERM), start_block), [((16, 24, TILE), F32)], vec)
    first = exchanged(part, DOC)
    part, row_scale = call(to_columns, (*tiles, first), [vector, scale], vec)
    part, col_scale = call(
        lambda *refs: left_product(docs, *refs),
        (*tiles, exchanged(part, TERM), first, start_block),
        [((RB, K, TILE), BF16), scale],
        [((CB, K + 16, TILE), BF16), ((RB, K + 16, TILE), F32)],
    )
    part, left_gram = call(
        left_rows, (exchanged(part, DOC), row_scale), [((16, K, TILE), BF16), ((K, K), F32)]
    )
    scaled = exchanged(part, DOC)
    half = (CB // 2, K + 16, TILE)
    keep, part = call(
        right_product,
        (*tiles, scaled, col_scale),
        [((CB // 2, K, TILE), F32), (half, jnp.int16)],
        [((CB, K, TILE), F32)],
    )
    part = lax.ppermute(part, "term_1", [(0, 1), (1, 0)])
    (part,) = call(core_sum, (keep, part), [(half, jnp.int16)], [((CB // 2, K, TILE), F32)])
    part, own = call(
        right_rows,
        (exchanged(part, "term_0"), left_gram),
        [((K, 3 * TILE), F32), ((K + 16, TILE), jnp.int16)],
    )
    part = exchanged(part.reshape(16, 16, 3 * TILE), DOC)
    (part,) = call(sum_docs, (part, own), [((LOW + 16, TILE), jnp.int16)])
    gathered = lax.all_gather(part, TERM)
    (part,) = call(sum_terms, (gathered,), [((16, 16, 3 * TILE), F32)])
    grams = exchanged(part, DOC).reshape(K, 3 * TILE)
    inverse, lean = call(
        lambda *refs: finish(terms, docs, *refs),
        (grams,),
        [((2, K, K), F32), ((K, TILE), F32)],
        [((2, K, 2 * K), F32)],
    )
    left_basis, right_basis = call(
        bases,
        (inverse, scaled, row_scale, gathered, lean),
        [((RB * TILE, K), BF16), ((CB * TILE, K), BF16)],
        [((RB * TILE, K), BF16), ((CB * TILE, K), BF16), pltpu.SemaphoreType.DMA((16,))],
        out_specs=[pl.BlockSpec(memory_space=pltpu.HBM)] * 2,
    )
    return (row_scale.reshape(-1), col_scale.reshape(-1), left_basis, right_basis)


def solution(mesh):
    torus = Mesh(mesh.devices.reshape(8, 2, 4, 4), ("term_0", "term_1", "doc_0", "doc_1"))
    placed = (P(TERM, DOC, None), P(TERM, DOC), P(TERM, DOC), P(TERM, DOC), P(DOC, None))
    return jax.shard_map(
        per_device,
        mesh=torus,
        in_specs=placed,
        out_specs=(P(TERM), P(DOC), P(TERM, None), P(DOC, None)),
        check_vma=False,
    )
```

```python
import jax
import jax.numpy as jnp
from jax import lax
from jax.experimental import pallas as pl
from jax.experimental.pallas import tpu as pltpu
from jax.sharding import Mesh
from jax.sharding import PartitionSpec as P

TILE = 128
K = 256
RB = 16
CB = 16
CAP = 48
GROUP = 24
PANEL = 64
TERM = ("term_0", "term_1")
DOC = ("doc_0", "doc_1")
F32 = jnp.float32
BF16 = jnp.bfloat16
PRECISE = lax.Precision.HIGHEST
VMEM = pl.BlockSpec(memory_space=pltpu.VMEM)
SMEM = pl.BlockSpec(memory_space=pltpu.SMEM)


def call(body, inputs, outs, scratch=(), specs=None, mib=16, out_specs=None):
    return pl.pallas_call(
        body,
        out_shape=[jax.ShapeDtypeStruct(s, d) for s, d in outs],
        in_specs=specs or [SMEM if a.dtype == jnp.int32 else VMEM for a in inputs],
        out_specs=out_specs or [VMEM] * len(outs),
        scratch_shapes=[pltpu.VMEM(s[0], s[1]) if isinstance(s, tuple) else s for s in scratch],
        compiler_params=pltpu.CompilerParams(vmem_limit_bytes=int(mib * 1024 * 1024)),
    )(*inputs)


def thirds(x):
    hi = x.astype(BF16)
    rest = x - hi.astype(F32)
    mid = rest.astype(BF16)
    low = (rest - mid.astype(F32)).astype(BF16)
    return hi, mid, low


def put_thirds(ref, vec, base):
    hi, mid, low = thirds(vec)
    row = lax.broadcasted_iota(jnp.int32, (16, TILE), 0)
    for b in range(RB):
        parts = [jnp.broadcast_to(p[b : b + 1].astype(F32), (16, TILE)) for p in (hi, mid, low)]
        rows = jnp.where(row == 0, parts[0], jnp.where(row == 1, parts[1], jnp.where(row == 2, parts[2], 0.0)))
        ref[b, base : base + 16, :] = rows.astype(BF16)


def over_tiles(count, values, source, target, src_ref, acc_ref, transposed, group, ready=None):
    acc_ref[...] = jnp.zeros(acc_ref.shape, F32)
    dims = (((1,), (1,)), ((), ())) if transposed else (((1,), (0,)), ((), ()))

    def visit(g, _):
        products = []
        for u in range(group):
            s = g * group + u
            tile = values[s]
            tile = jnp.where(s < count, tile, jnp.zeros_like(tile))
            products.append(
                lax.dot_general(src_ref[source[0, s]], tile, dims, preferred_element_type=F32)
            )
        for u in range(group):
            s = g * group + u
            acc_ref[target[0, s]] += products[u]
        return 0

    if ready is None and group < CAP:
        lax.fori_loop(0, (count + group - 1) // group, visit, 0)
        return
    for g in range(CAP // group):
        if ready is not None:
            ready(g)
        visit(g, 0)


def send_vector(out_ref, acc_ref):
    vec = jnp.sum(acc_ref[...], axis=1)
    for i in range(16):
        out_ref[i, 0:RB, :] = vec


def first_rows(values_in, rows_in, cols_in, count, out, src, acc, values, rows, cols, sems):
    parts = CAP // GROUP
    copies = [pltpu.make_async_copy(rows_in, rows, sems.at[0]), pltpu.make_async_copy(cols_in, cols, sems.at[1])]
    for g in range(parts):
        own = pl.ds(g * GROUP, GROUP)
        copies.append(pltpu.make_async_copy(values_in.at[own], values.at[own], sems.at[2 + g]))
    for copy in copies:
        copy.start()
    put_thirds(src, jnp.ones((CB, TILE), F32), 0)
    copies[0].wait()
    copies[1].wait()
    over_tiles(count[0, 0], values, cols, rows, src, acc, True, GROUP, lambda g: copies[2 + g].wait())
    send_vector(out, acc)


def to_columns(values, rows, cols, count, got, out, scale, src, acc):
    vec = 1.0 / jnp.sum(got[...], axis=0)[0:RB]
    scale[...] = vec
    put_thirds(src, vec, 0)
    over_tiles(count[0, 0], values, rows, cols, src, acc, False, CAP)
    send_vector(out, acc)


def to_rows(values, rows, cols, count, got, start, out, src, acc):
    put_thirds(src, 1.0 / jnp.sum(got[...], axis=0), 0)
    over_tiles(count[0, 0], values, cols, rows, src, acc, True, GROUP)
    send_vector(out, acc)
    mean = jnp.sum(start[...].astype(F32), axis=0, keepdims=True)
    for i in range(16):
        out[i, 16:17, :] = mean[:, :TILE]
        out[i, 17:18, :] = mean[:, TILE:]
        out[i, 18:24, :] = jnp.zeros((6, TILE), F32)


def left_product(docs, values, rows, cols, count, got, first, start, out, scale, src, acc):
    vec = 1.0 / jnp.sum(got[...], axis=0)
    scale[...] = vec
    put_thirds(src, vec, K)
    for b in range(CB):
        block = start[b * TILE : (b + 1) * TILE, :].T.astype(F32)
        src[b, 0:K, :] = (block * vec[b : b + 1, :]).astype(BF16)
    mean = jnp.sum(first[...], axis=0)[16:18] / docs
    mean = jnp.concatenate([jnp.broadcast_to(mean[h : h + 1], (TILE, TILE)).T for h in range(2)], axis=0)
    over_tiles(count[0, 0], values, cols, rows, src, acc, True, GROUP)
    for b in range(RB):
        weight = jnp.sum(acc[b, K : K + 16, :], axis=0, keepdims=True)
        out[b] = (acc[b, 0:K, :] - mean * weight).astype(out.dtype)


def left_rows(got, row_scale, out, gram):
    d = lax.axis_index(DOC)
    scale = row_scale[pl.ds(d, 1), :]
    left = scale * jnp.sum(got[...].astype(F32), axis=0)
    sent = (left * scale).astype(BF16)
    for i in range(16):
        out[i] = sent
    gram[...] = lax.dot_general(left, left, (((1,), (1,)), ((), ())), precision=PRECISE, preferred_element_type=F32)


LEVELS = 32000.0
STEPS = 64.0


def code_of(peak):
    return jnp.ceil(jnp.log2(jnp.maximum(peak, 1e-37)) * STEPS)


def code_lines(code):
    lines = jnp.broadcast_to(code, (K, TILE)).T
    return jnp.concatenate([lines[0:8, :TILE], lines[0:8, TILE:]], axis=0).astype(jnp.int32).astype(jnp.int16)


def counted(x, code):
    steps = x * (jnp.exp2(code * (-1.0 / STEPS)) * LEVELS)
    return jnp.floor(steps + 0.5).astype(jnp.int32).astype(jnp.int16)


def wide(x):
    return x.astype(jnp.int32).astype(F32)


def steps_of(got, count):
    lines = [wide(got[i, K : K + 16, :]) for i in range(count)]
    code = jnp.concatenate(
        [jnp.concatenate([x[h : h + 1] for x in lines], axis=0) for h in (0, 8)], axis=1
    ).T
    return jnp.exp2(code * (1.0 / STEPS)) * (1.0 / LEVELS)


def right_product(values, rows, cols, count, scaled, col_scale, keep, send, acc):
    over_tiles(count[0, 0], values, rows, cols, scaled, acc, False, GROUP)
    core = lax.axis_index("term_1")
    peak = jnp.zeros((K, TILE), F32)
    for i in range(CB // 2):
        mine, its = 2 * i + core, 2 * i + 1 - core
        keep[i] = acc[mine] * col_scale[pl.ds(mine, 1), :]
        part = acc[its] * col_scale[pl.ds(its, 1), :]
        acc[its] = part
        peak = jnp.maximum(peak, jnp.abs(part))
    code = code_of(jnp.max(peak, axis=1, keepdims=True))
    lines = code_lines(code)
    for i in range(CB // 2):
        send[i, 0:K, :] = counted(acc[2 * i + 1 - core], code)
        send[i, K : K + 16, :] = lines


def core_sum(keep, got, out, total):
    step = steps_of(got, 8)[:, 0:1]
    peak = jnp.zeros((K, TILE), F32)
    for i in range(CB // 2):
        part = keep[i] + wide(got[i, 0:K, :]) * step
        total[i] = part
        peak = jnp.maximum(peak, jnp.abs(part))
    code = code_of(jnp.max(peak, axis=1, keepdims=True))
    lines = code_lines(code)
    for i in range(CB // 2):
        out[i, 0:K, :] = counted(total[i], code)
        out[i, K : K + 16, :] = lines


def iotas(shape=(K, K)):
    return lax.broadcasted_iota(jnp.int32, shape, 0), lax.broadcasted_iota(jnp.int32, shape, 1)


def right_rows(got, left_gram, out, own):
    step = steps_of(got, 8)
    right = wide(got[0, 0:K, :]) * step[:, 0:1]
    for i in range(1, 8):
        right += wide(got[i, 0:K, :]) * step[:, i : i + 1]
    code = code_of(jnp.max(jnp.abs(right), axis=1, keepdims=True))
    own[0:K, :] = counted(right, code)
    own[K : K + 16, :] = code_lines(code)
    gram = lax.dot_general(right, right, (((1,), (1,)), ((), ())), precision=PRECISE, preferred_element_type=F32)
    row, col = iotas()
    packed = jnp.where(row >= col, left_gram[...], gram)
    diag = jnp.sum(jnp.where(row == col, gram, 0.0), axis=1, keepdims=True)
    lean = jnp.sum(right, axis=1, keepdims=True)
    lane = lax.broadcasted_iota(jnp.int32, (K, TILE), 1)
    extra = jnp.where(lane == 0, diag, jnp.where(lane == 1, lean, 0.0))
    out[:, 0:K] = packed
    out[:, K : K + TILE] = extra


FINE = 64000.0
OWN = K + 16
MID = OWN + 48
LOW = MID + 48


def sum_docs(got, own, out):
    out[0:OWN, :] = own[...]
    total = jnp.sum(got[...], axis=0)
    code = code_of(jnp.max(jnp.abs(total), axis=1, keepdims=True))
    steps = total * (jnp.exp2(code * (-1.0 / STEPS)) * LEVELS)
    whole = jnp.floor(steps + 0.5)
    part = jnp.floor((steps - whole) * FINE + 0.5)
    for h in range(3):
        lanes = slice(h * TILE, (h + 1) * TILE)
        out[OWN + 16 * h : OWN + 16 * h + 16, :] = whole[:, lanes].astype(jnp.int32).astype(jnp.int16)
        out[MID + 16 * h : MID + 16 * h + 16, :] = part[:, lanes].astype(jnp.int32).astype(jnp.int16)
    out[LOW : LOW + 16, :] = jnp.broadcast_to(code, (16, TILE)).astype(jnp.int32).astype(jnp.int16)


def sum_terms(got, out):
    total = [jnp.zeros((16, TILE), F32)] * 3
    for i in range(16):
        step = jnp.exp2(wide(got[i, LOW : LOW + 16, :]) * (1.0 / STEPS)) * (1.0 / LEVELS)
        for h in range(3):
            whole = wide(got[i, OWN + 16 * h : OWN + 16 * h + 16, :])
            part = wide(got[i, MID + 16 * h : MID + 16 * h + 16, :])
            total[h] = total[h] + (whole + part * (1.0 / FINE)) * step
    total = jnp.concatenate(total, axis=1)
    for i in range(16):
        out[i] = total


def spread(x, lane):
    return jnp.broadcast_to(x[:, :, lane : lane + 1], x.shape)


def eliminate(blocks, at):
    blocks = [list(b) for b in blocks]
    sub = lax.broadcasted_iota(jnp.int32, (2, 8, TILE), 1)
    for g in range(len(blocks)):
        lead = blocks[g]
        lanes = [at + 8 * g + b for b in range(8)]
        head = [spread(lead[0], l) for l in lanes]
        pivots = jnp.ones((2, 8, TILE), F32)
        lines, inverses, entries = [], [], []
        for a in range(8):
            pivot = head[a][:, a : a + 1]
            inv = 1.0 / pivot
            line = [x[:, a : a + 1] for x in lead]
            entry = [head[b][:, a : a + 1] for b in range(8)]
            lines.append(line)
            inverses.append(inv)
            entries.append(entry)
            pivots = jnp.where(sub == a, pivot, pivots)
            f = jnp.where(sub > a, head[a], 0.0) * inv
            lead = [x - f * y for x, y in zip(lead, line)]
            for b in range(a + 1, 8):
                head[b] = head[b] - f * entry[b]
        for j in range(g + 1, len(blocks)):
            cols = [spread(blocks[j][0], l) for l in lanes]
            total = blocks[j]
            for a in range(8):
                f = cols[a] * inverses[a]
                total = [x - f * y for x, y in zip(total, lines[a])]
                for b in range(a + 1, 8):
                    cols[b] = cols[b] - f * entries[a][b]
            blocks[j] = total
        root = lax.rsqrt(pivots)
        blocks[g] = [x * root for x in lead]
    return blocks


def precise(lhs, rhs, contract=1):
    return lax.dot_general(lhs, rhs, (((contract,), (0,)), ((), ())), precision=PRECISE, preferred_element_type=F32)


def factor(work):
    lane = lax.broadcasted_iota(jnp.int32, (2, PANEL, TILE), 2)
    line = lax.broadcasted_iota(jnp.int32, (2, PANEL, TILE), 1)
    own = work[:, 0:PANEL, 0:TILE]
    for start in range(0, K, PANEL):
        first = (start // TILE) * TILE
        end = start + PANEL
        span = slice(first if end < K else K, first + 3 * TILE)
        at = start - first
        other = PANEL - at
        unit = jnp.where(lane == line + other, 1.0, 0.0)
        here = (lane >= at) & (lane < at + PANEL)
        parts = [jnp.where(here, own, unit)]
        then = (end // TILE) * TILE
        if end < K:
            parts.append(own if then == first else work[:, start:end, then : then + TILE])
        done = eliminate([[x[:, 8 * j : 8 * j + 8] for x in parts] for j in range(PANEL // 8)], at)
        done = [jnp.concatenate([b[i] for b in done], axis=1) for i in range(len(parts))]
        inverses = [done[0][m, :, other : other + PANEL] for m in range(2)]
        if end < K:
            ahead = []
            for m in range(2):
                upper = done[1][m]
                cut = upper[:, end - then : end - then + PANEL]
                ahead.append(work[m, end : end + PANEL, then : then + TILE] - precise(cut, upper, 0))
            own = jnp.stack(ahead)
        for m in range(2):
            panel = precise(inverses[m], work[m, start:end, span])
            work[m, start:end, span] = panel
            if end < K:
                work[m, end:K, span] -= precise(panel[:, end - first : K - first], panel, 0)


def finish(terms, docs, grams, inverse, lean_out, work):
    row, col = iotas()
    one = grams[:, 0:K]
    other = one.T
    e = grams[:, K : K + TILE]
    lean = e[:, 1:2] / docs
    lean_row = jnp.sum(jnp.where(row == col, lean, 0.0), axis=0, keepdims=True)
    left = jnp.where(row >= col, one, other) / terms
    right = jnp.where(row < col, one, jnp.where(row == col, e[:, 0:1], other)) / docs - lean * lean_row
    eye = jnp.where(row == col, 1.0, 0.0).astype(F32)
    for m, gram in ((0, left), (1, right)):
        work[m, :, 0:K] = gram
        work[m, :, K : 2 * K] = eye
    factor(work)
    for m in range(2):
        inverse[m] = jnp.where(row >= col, work[m, :, K : 2 * K], 0.0)
    lean_out[...] = jnp.broadcast_to(lean, lean_out.shape)


def halves(x):
    hi = x.astype(BF16)
    return hi, (x - hi.astype(F32)).astype(BF16)


def mixed(lhs, rhs):
    return sum(jnp.dot(a, b, preferred_element_type=F32) for a, b in zip(lhs, rhs))


def bases(inverse, scaled, row_scale, gathered, lean, left_out, right_out, left_held, right_held, sems):
    copies = []

    def send(rows, out, b):
        own = pl.ds(b * TILE, 2 * TILE)
        copies.append(pltpu.make_async_copy(rows.at[own], out.at[own], sems.at[len(copies)]))
        copies[-1].start()

    hi, low = halves(inverse[0])
    for b in range(0, RB, 2):
        pair = jnp.concatenate([scaled[b], scaled[b + 1]], axis=1)
        total = mixed((hi, low), (pair, pair))
        for u in range(2):
            basis = total[:, u * TILE : (u + 1) * TILE] / row_scale[b + u : b + u + 1, :]
            left_held[(b + u) * TILE : (b + u + 1) * TILE, :] = basis.T.astype(BF16)
        send(left_held, left_out, b)
    hi, low = halves(inverse[1])
    step = steps_of(gathered, 16)
    mean = lean[:, 0:1]
    for b in range(0, CB, 2):
        pair = jnp.concatenate(
            [wide(gathered[b + u, 0:K, :]) * step[:, b + u : b + u + 1] - mean for u in range(2)], axis=1
        )
        top, rest = halves(pair)
        total = mixed((hi, low, hi), (top, top, rest))
        for u in range(2):
            right_held[(b + u) * TILE : (b + u + 1) * TILE, :] = total[:, u * TILE : (u + 1) * TILE].T.astype(BF16)
        send(right_held, right_out, b)
    for copy in copies:
        copy.wait()


def exchanged(x, axis):
    return lax.all_to_all(x, axis, split_axis=0, concat_axis=0, tiled=True)


def per_device(tile_values, tile_rows, tile_cols, tile_count, start_block):
    terms = float(RB * TILE * lax.axis_size(TERM))
    docs = float(CB * TILE * lax.axis_size(DOC))
    tiles = (tile_values, tile_rows, tile_cols, tile_count)
    vec = [((RB, 16, TILE), BF16), ((RB, 16, TILE), F32)]
    vector = ((16, RB, TILE), F32)
    scale = ((RB, TILE), F32)
    lists = pltpu.SMEM((1, CAP), jnp.int32)
    (part,) = call(
        first_rows,
        tiles,
        [vector],
        [*vec, (tile_values.shape, BF16), lists, lists, pltpu.SemaphoreType.DMA((2 + CAP // GROUP,))],
        [pl.BlockSpec(memory_space=pltpu.HBM)] * 3 + [SMEM],
        60,
    )
    part, _ = call(to_columns, (*tiles, exchanged(part, DOC)), [vector, scale], vec)
    (part,) = call(to_rows, (*tiles, exchanged(part, TERM), start_block), [((16, 24, TILE), F32)], vec)
    first = exchanged(part, DOC)
    part, row_scale = call(to_columns, (*tiles, first), [vector, scale], vec)
    part, col_scale = call(
        lambda *refs: left_product(docs, *refs),
        (*tiles, exchanged(part, TERM), first, start_block),
        [((RB, K, TILE), BF16), scale],
        [((CB, K + 16, TILE), BF16), ((RB, K + 16, TILE), F32)],
    )
    part, left_gram = call(
        left_rows, (exchanged(part, DOC), row_scale), [((16, K, TILE), BF16), ((K, K), F32)]
    )
    scaled = exchanged(part, DOC)
    half = (CB // 2, K + 16, TILE)
    keep, part = call(
        right_product,
        (*tiles, scaled, col_scale),
        [((CB // 2, K, TILE), F32), (half, jnp.int16)],
        [((CB, K, TILE), F32)],
    )
    part = lax.ppermute(part, "term_1", [(0, 1), (1, 0)])
    (part,) = call(core_sum, (keep, part), [(half, jnp.int16)], [((CB // 2, K, TILE), F32)])
    part, own = call(
        right_rows,
        (exchanged(part, "term_0"), left_gram),
        [((K, 3 * TILE), F32), ((K + 16, TILE), jnp.int16)],
    )
    part = exchanged(part.reshape(16, 16, 3 * TILE), DOC)
    (part,) = call(sum_docs, (part, own), [((LOW + 16, TILE), jnp.int16)])
    gathered = lax.all_gather(part, TERM)
    (part,) = call(sum_terms, (gathered,), [((16, 16, 3 * TILE), F32)])
    grams = exchanged(part, DOC).reshape(K, 3 * TILE)
    inverse, lean = call(
        lambda *refs: finish(terms, docs, *refs),
        (grams,),
        [((2, K, K), F32), ((K, TILE), F32)],
        [((2, K, 2 * K), F32)],
    )
    left_basis, right_basis = call(
        bases,
        (inverse, scaled, row_scale, gathered, lean),
        [((RB * TILE, K), BF16), ((CB * TILE, K), BF16)],
        [((RB * TILE, K), BF16), ((CB * TILE, K), BF16), pltpu.SemaphoreType.DMA((16,))],
        out_specs=[pl.BlockSpec(memory_space=pltpu.HBM)] * 2,
    )
    return (row_scale.reshape(-1), col_scale.reshape(-1), left_basis, right_basis)


def solution(mesh):
    torus = Mesh(mesh.devices.reshape(8, 2, 4, 4), ("term_0", "term_1", "doc_0", "doc_1"))
    placed = (P(TERM, DOC, None), P(TERM, DOC), P(TERM, DOC), P(TERM, DOC), P(DOC, None))
    return jax.shard_map(
        per_device,
        mesh=torus,
        in_specs=placed,
        out_specs=(P(TERM), P(DOC), P(TERM, None), P(DOC, None)),
        check_vma=False,
    )
```
